256 devices in a mesh: req: 8 (over z), head: 2 (over core), exp: 16 (over x, y).
Axes of the slice: x: 4, y: 4, z: 8, core: 2. Of those that a mesh axis runs over, the one named last changes fastest.
Arguments:
- queries: bfloat16 [32, 64, 32, 128], P('req', 'exp', 'head'), may hold values from -8 to 8
- new_keys: bfloat16 [32, 64, 4, 128], P('req', 'exp', 'head'), may hold values from -8 to 8
- new_values: bfloat16 [32, 64, 4, 128], P('req', 'exp', 'head'), may hold values from -6 to 6
- key_cache: bfloat16 [32, 24576, 4, 128], P('req', 'exp', 'head'), may hold values from -6 to 6
- value_cache: bfloat16 [32, 24576, 4, 128], P('req', 'exp', 'head'), may hold values from -6 to 6
- lengths: int32 [32], P('req'), may hold values from 1 to 24576, 262144 in all
- residual: bfloat16 [2048, 2048], P(('req', 'exp')), may hold values from -24 to 24
- out_weight: bfloat16 [4096, 2048], P('head', 'exp'), may hold values from -1.796875 to 1.796875
- norm_gain: float32 [2048], replicated, may hold values from 0.1 to 1.9
- route_ids: int32 [2048, 8], P(('req', 'exp')), may hold values from 0 to 127, all different within a row; in each aligned block of 16 rows (0 to 15, 16 to 31, ...) at most 2 rows name the same one
- route_weights: float32 [2048, 8], P(('req', 'exp')), may hold values from 0.05 to 0.3
- expert_in: bfloat16 [128, 2048, 2, 768], P(('req', 'exp'), None, None, 'head'), may hold values from -0.125 to 0.125
- expert_out: bfloat16 [128, 768, 2048], P(('req', 'exp'), 'head'), may hold values from -0.21875 to 0.21875
Outputs:
- output: bfloat16 [2048, 2048], P(('req', 'exp'), 'head')
The draws below stay inside these ranges and needn't reach their ends.
Inputs may be any that keep to these rules, and one draw needn't show every extreme that they name: `route_ids`: each row names 8 different experts. Among the 16 rows of one device (aligned blocks of rows 0 to 15, 16 to 31 and so on) no expert is named by more than 2 rows.
All inputs are finite; a program needn't handle non-finite values. No bound on the sum of `lengths` on one device may be relied on, other than what follows from the above.
Results may differ from the reference program's by a relative error of at most 0.0051.
Values may be sent and summed in bfloat16 or wider, within the bound.
A program may use at most 128 MiB of HBM per device.

```python
import math
import jax
import jax.numpy as jnp
import numpy as np
from jax import lax

D = 2048
H = 32
KVH = 4
HD = 128
FF = 768
TOPK = 8
EXPERTS = 128
BLOCK = 64
MAXLEN = 24576
MEAN_LEN = 8192
REQUESTS = 32
TOKENS = 2048
ROWS_DEV = 16
CAP = 2


def draw_queries(key, part):
    values = 1.5 * jax.random.normal(jax.random.fold_in(key, 11), (REQUESTS, BLOCK, H, HD), jnp.float32)
    values = jnp.clip(values, -8.0, 8.0)
    return values.astype(jnp.bfloat16)


def draw_new_keys(key, part):
    values = 2.0 * jax.random.normal(jax.random.fold_in(key, 23), (REQUESTS, BLOCK, KVH, HD), jnp.float32)
    values = jnp.clip(values, -8.0, 8.0)
    return values.astype(jnp.bfloat16)


def draw_residual(key, part):
    row_scales = jnp.exp(jax.random.uniform(jax.random.fold_in(key, 31), (TOKENS, 1), jnp.float32, math.log(0.3), math.log(3.0)))
    column_scales = jnp.exp(jax.random.uniform(jax.random.fold_in(key, 32), (1, D), jnp.float32, math.log(0.2), math.log(2.0)))
    base_values = jnp.clip(jax.random.normal(jax.random.fold_in(key, 33), (TOKENS, D), jnp.float32), -4.0, 4.0)
    return (base_values * row_scales * column_scales).astype(jnp.bfloat16)


def block_scale(own_key, shape, shards, smallest, top_value):
    def one(position, parts):
        draws = jax.random.uniform(jax.random.fold_in(jax.random.fold_in(own_key, 6), position), (parts,), jnp.float32, smallest / len(shards), top_value / len(shards))
        return jnp.repeat(jnp.exp(draws), shape[position] // parts).reshape((-1,) + (1,) * (len(shape) - position - 1))

    loudness = one(*shards[0])
    for cut in shards[1:]:
        loudness = loudness * one(*cut)
    return loudness


def split_up(number_of, total, most, slope):
    loads = [(1 << 20) // math.isqrt(rank ** slope) + 1 for rank in range(2, number_of + 1)]
    surplus, counts = total - most - (number_of - 1), [1] * (number_of - 1)
    while surplus > 0:
        movable = [i for i in range(number_of - 1) if counts[i] < most]
        mass, left = sum([loads[i] for i in movable]), surplus
        for i in movable:
            more = min(most - counts[i], max(1, left * loads[i] // mass), surplus)
            counts[i] = counts[i] + more
            surplus = surplus - more
    return np.array([most] + counts)


def ragged(rng, count, total, most, lean):
    if count == 2:
        one = jax.random.randint(rng, (), max(1, total - most), min(most, total - 1) + 1)
        return jnp.stack([one, total - one])
    tallies = jnp.asarray(split_up(count, total, most, lean), jnp.int32)
    twos = (count - 1) // 2
    giver, receiver = tallies[1:1 + 2 * twos:2], tallies[2:2 + 2 * twos:2]
    slack = jnp.minimum(giver - 1, most - receiver)
    shifted = jax.random.randint(jax.random.fold_in(rng, 1), (twos,), 0, 1 << 20) % (slack + 1)
    tallies = tallies.at[1:1 + 2 * twos:2].set(giver - shifted).at[2:2 + 2 * twos:2].set(receiver + shifted)
    return tallies[jax.random.permutation(jax.random.fold_in(rng, 2), count)]


def shared_out(key, own, number, rows, count, top, reach, slope):
    order = jax.random.permutation(key, count)
    heavy_load, common = portions_of(count, rows * top, reach, slope, True), portions_of(count, rows * top, reach, slope, False)
    places = jnp.arange(count)

    def named(sizes, turn):
        used = int((sizes > 0).sum())
        fixed = max(1, used // 4)
        shifted = fixed + (places - fixed + turn * (used - fixed)) % max(1, count - fixed)
        return jnp.zeros((count,), jnp.int32).at[order[jnp.where(places < fixed, places, shifted)]].set(jnp.asarray(sizes, jnp.int32))

    sizes = jnp.where(number % 4 == 0, named(heavy_load, number // 4), named(common, number - number // 4 - 1))
    mixed = jax.random.permutation(jax.random.fold_in(own, 3), count)
    source_of, sink = mixed[0:count // 2 * 2:2], mixed[1:count // 2 * 2:2]
    slack = jnp.minimum(sizes[source_of] - 1, reach - sizes[sink]) // 2
    slack = jnp.where((source_of == order[0]) | (sink == order[0]) | (sizes[sink] == 0), 0, jnp.maximum(slack, 0))
    shifted = jax.random.randint(jax.random.fold_in(own, 4), (count // 2,), 0, 1 << 20) % (slack + 1)
    sizes = sizes.at[source_of].add(-shifted).at[sink].add(shifted)
    labels = jnp.searchsorted(jnp.cumsum(sizes), jnp.arange(rows * top), side="right").astype(jnp.int32)
    table = labels.reshape(top, rows).T
    table = table[jax.random.permutation(jax.random.fold_in(own, 1), rows)]
    turn = jax.random.randint(jax.random.fold_in(own, 2), (rows, 1), 0, top)
    return jnp.take_along_axis(table, (jnp.arange(top)[None, :] + turn) % top, axis=1)


def portions_of(number_of, total, reach, skew, full):
    weights = [(1 << 20) // math.isqrt(rank ** skew) + 1 for rank in range(1, number_of + 1)]
    largest = reach if full else min(reach, max(-(-total // number_of), total * weights[0] // sum(weights)))
    least = 1 if total - largest >= number_of - 1 else 0
    counts, rest = [largest] + [least] * (number_of - 1), total - largest - least * (number_of - 1)
    while rest > 0:
        candidates = [i for i in range(1, number_of) if counts[i] < largest] or [i for i in range(1, number_of) if counts[i] < reach]
        pool, budget = sum([weights[i] for i in candidates]), rest
        for i in candidates:
            more = min(reach - counts[i], max(1, budget * weights[i] // pool), rest)
            counts[i] = counts[i] + more
            rest = rest - more
    return np.array(counts)


def gaussian(rng, dims, width, most, pieces=(), kind=jnp.bfloat16):
    loudness = block_scale(rng, dims, pieces, -0.22, 0.18) if pieces else 1.0
    values = jax.random.normal(rng, dims, jnp.float32) * width * loudness
    return jnp.minimum(jnp.maximum(values, -most), most).astype(kind)


def setup_inputs(seed: int = 0) -> dict:
    splits = jax.random.split(jax.random.key(seed), 14)
    queries = draw_queries(jax.random.fold_in(splits[13], 71), 0)
    new_keys = draw_new_keys(jax.random.fold_in(splits[13], 71), 0)
    new_values = gaussian(splits[2], (REQUESTS, BLOCK, KVH, HD), 1.0, 6.0, ((0, 8), (1, 16), (2, 2)))
    key_cache = gaussian(splits[3], (REQUESTS, MAXLEN, KVH, HD), 1.0, 6.0, ((0, 8), (1, 16), (2, 2)))
    value_cache = gaussian(splits[4], (REQUESTS, MAXLEN, KVH, HD), 1.0, 6.0, ((0, 8), (1, 16), (2, 2)))
    lengths = ragged(splits[5], REQUESTS, REQUESTS * MEAN_LEN, MAXLEN, 2).astype(jnp.int32)
    residual = draw_residual(jax.random.fold_in(splits[13], 71), 0)
    out_weight = gaussian(splits[7], (H * HD, D), 0.3, 1.796875, ((0, 2), (1, 16)))
    norm_gain = jnp.clip(1.0 + 0.18 * jax.random.normal(splits[8], (D,), jnp.float32), 0.1, 1.9)
    route_ids_keys = jax.random.split(jax.random.fold_in(splits[9], 1), TOKENS // ROWS_DEV)
    route_ids_turns = jax.random.permutation(jax.random.fold_in(splits[9], 3), TOKENS // ROWS_DEV)
    route_ids = jax.vmap(lambda own, number: shared_out(jax.random.fold_in(splits[9], 2), own, number, ROWS_DEV, EXPERTS, TOPK, CAP, 2))(route_ids_keys, route_ids_turns).reshape((TOKENS, TOPK))
    route_weights = jnp.clip(0.05 + 0.25 * jax.random.uniform(splits[10], (TOKENS, TOPK), jnp.float32) ** block_scale(splits[10], (TOKENS, TOPK), ((0, 128),), -0.2, 0.2), 0.05, 0.3)
    expert_in = gaussian(splits[11], (EXPERTS, D, 2, FF), D ** -0.5, 0.125, ((0, 128), (3, 2)))
    expert_out = gaussian(splits[12], (EXPERTS, FF, D), FF ** -0.5, 0.21875, ((0, 128), (1, 2)))
    return dict(queries=queries, new_keys=new_keys, new_values=new_values, key_cache=key_cache, value_cache=value_cache, lengths=lengths, residual=residual, out_weight=out_weight, norm_gain=norm_gain, route_ids=route_ids, route_weights=route_weights, expert_in=expert_in, expert_out=expert_out)


masked_score = -1e+30
norm_epsilon = 1e-06

def attend(operands):
    query, new_key, new_value, cached_key, cached_value, length = operands
    group_size = H // KVH
    query_rows = query.astype(jnp.float32).reshape(BLOCK, KVH, group_size, HD)
    all_keys = jnp.concatenate([cached_key, new_key], axis=0).astype(jnp.float32)
    all_values = jnp.concatenate([cached_value, new_value], axis=0).astype(jnp.float32)
    positions = jnp.arange(MAXLEN + BLOCK, dtype=jnp.int32)
    included = (positions < length) | (positions >= MAXLEN)
    scores = jnp.einsum('bkgd,skd->kgbs', query_rows, all_keys) * HD ** (-0.5)
    scores = jnp.where(included, scores, masked_score)
    row_max = lax.optimization_barrier(jnp.max(scores, axis=-1, keepdims=True))
    exponent = jnp.exp(scores - row_max)
    totals = lax.optimization_barrier(jnp.sum(exponent, axis=-1))
    rounded = lax.optimization_barrier(exponent.astype(jnp.bfloat16)).astype(jnp.float32)
    summed = jnp.einsum('kgbs,skd->bkgd', rounded, all_values)
    result = summed / jnp.transpose(totals, (2, 0, 1))[..., None]
    return result.reshape(BLOCK, H * HD).astype(jnp.bfloat16)

def reference(queries, new_keys, new_values, key_cache, value_cache, lengths, residual, out_weight, norm_gain, route_ids, route_weights, expert_in, expert_out):
    attn = lax.map(attend, (queries, new_keys, new_values, key_cache, value_cache, lengths))
    attn = attn.reshape(TOKENS, H * HD)
    projected = jnp.dot(attn, out_weight, preferred_element_type=jnp.float32)
    hidden = residual.astype(jnp.float32) + projected
    normed = (hidden * lax.rsqrt(lax.optimization_barrier(jnp.mean(hidden * hidden, axis=-1, keepdims=True)) + norm_epsilon) * norm_gain).astype(jnp.bfloat16)
    load_cap = TOKENS // ROWS_DEV * CAP
    padded_rows = jnp.concatenate([normed, jnp.zeros((1, D), jnp.bfloat16)], axis=0)

    def one_expert(accumulated, expert_id):
        hit_mask = route_ids == expert_id
        routed = jnp.any(hit_mask, axis=1)
        weight_row = lax.optimization_barrier(jnp.sum(jnp.where(hit_mask, route_weights, jnp.float32(0.0)), axis=1))
        weight_row = jnp.concatenate([weight_row, jnp.zeros((1,), jnp.float32)])
        selected = jnp.nonzero(routed, size=load_cap, fill_value=TOKENS)[0]
        gathered_rows = padded_rows[selected]
        gate_up = jnp.dot(gathered_rows, expert_in[expert_id].reshape(D, 2 * FF), preferred_element_type=jnp.float32)
        activated = (jax.nn.silu(gate_up[:, :FF]) * gate_up[:, FF:]).astype(jnp.bfloat16)
        result = jnp.dot(activated, expert_out[expert_id], preferred_element_type=jnp.float32).astype(jnp.bfloat16)
        accumulated = accumulated.at[selected].add(weight_row[selected][:, None] * result.astype(jnp.float32))
        return (accumulated, None)
    mixture, unused = lax.scan(one_expert, jnp.zeros((TOKENS + 1, D), jnp.float32), jnp.arange(EXPERTS, dtype=jnp.int32))
    return (hidden + mixture[:TOKENS]).astype(jnp.bfloat16)
```

```python
import jax
import jax.numpy as jnp
from jax import lax
from jax.sharding import PartitionSpec as P

masked_score = -1e30
norm_epsilon = 1e-06


def normalize(value_sums, row_totals, heads_local):
    lead = value_sums.shape[:2]
    shaped = value_sums.reshape(lead[0], lead[1], heads_local, -1) / row_totals[..., None]
    return shaped.reshape(lead[0], lead[1], -1).astype(jnp.bfloat16)


def local(
    queries,
    new_keys,
    new_values,
    key_cache,
    value_cache,
    lengths,
    residual,
    out_weight,
    norm_gain,
    route_ids,
    route_weights,
    expert_in,
    expert_out,
):
    req_count, cache_span, kv_local, head_size = key_cache.shape
    heads_local = queries.shape[2]
    group_size = heads_local // kv_local
    score_scale = head_size ** (-0.5)
    whole_queries = lax.all_gather(queries, "exp", axis=1, tiled=True)
    block_rows = whole_queries.shape[1]
    grouped = whole_queries.reshape(req_count, block_rows, kv_local, group_size, head_size)
    cache_scores = (
        jnp.einsum("rbkgd,rskd->rkgbs", grouped, key_cache, preferred_element_type=jnp.float32)
        * score_scale
    )
    fresh_scores = (
        jnp.einsum("rbkgd,rnkd->rkgbn", grouped, new_keys, preferred_element_type=jnp.float32)
        * score_scale
    )
    positions = lax.axis_index("exp") * cache_span + lax.iota(jnp.int32, cache_span)
    valid_cache = positions[None, :] < lengths[:, None]
    cache_scores = jnp.where(valid_cache[:, None, None, None, :], cache_scores, masked_score)
    local_max = jnp.maximum(jnp.max(cache_scores, axis=-1), jnp.max(fresh_scores, axis=-1))
    row_max = lax.pmax(local_max, "exp")
    cache_exp = jnp.exp(cache_scores - row_max[..., None])
    fresh_exp = jnp.exp(fresh_scores - row_max[..., None])
    totals = jnp.sum(cache_exp, axis=-1) + jnp.sum(fresh_exp, axis=-1)
    weighted = jnp.einsum(
        "rkgbs,rskd->rbkgd",
        cache_exp.astype(jnp.bfloat16),
        value_cache,
        preferred_element_type=jnp.float32,
    )
    weighted = weighted + jnp.einsum(
        "rkgbn,rnkd->rbkgd",
        fresh_exp.astype(jnp.bfloat16),
        new_values,
        preferred_element_type=jnp.float32,
    )
    weighted = weighted.reshape(req_count, block_rows, heads_local * head_size)
    totals = jnp.transpose(totals, (0, 3, 1, 2)).reshape(req_count, block_rows, heads_local)
    all_sums, all_totals = lax.psum((weighted, totals), "exp")
    merged = normalize(all_sums, all_totals, heads_local)
    projected = jnp.dot(
        merged.reshape(req_count * block_rows, -1), out_weight, preferred_element_type=jnp.float32
    )
    projected = projected.reshape(req_count, block_rows, -1)
    projected = lax.psum(projected, "head")
    projected = projected.reshape(req_count * block_rows, projected.shape[-1])
    attn_out = lax.all_to_all(projected, "exp", split_axis=0, concat_axis=1, tiled=True)
    hidden = residual.astype(jnp.float32) + attn_out
    normed = (
        hidden
        * lax.rsqrt(jnp.mean(hidden * hidden, axis=-1, keepdims=True) + norm_epsilon)
        * norm_gain
    ).astype(jnp.bfloat16)
    row_count, model_width = normed.shape
    top_count = route_ids.shape[1]
    local_experts = expert_in.shape[0]
    groups = lax.axis_size("req") * lax.axis_size("exp")
    experts_all = local_experts * groups
    capacity = max(2, 2 * row_count * top_count // experts_all)
    expert_iota = lax.iota(jnp.int32, experts_all)
    named_count = jnp.sum((route_ids[:, :, None] == expert_iota).astype(jnp.int32), axis=1)
    row_iota = lax.iota(jnp.int32, row_count)
    before = (row_iota[None, :] < row_iota[:, None]).astype(jnp.int32)
    earlier = jnp.sum(before[:, :, None] * named_count[None], axis=1)
    slot_rank = jnp.take_along_axis(earlier, route_ids, axis=1)
    slot_index = route_ids * capacity + slot_rank
    slot_iota = lax.iota(jnp.int32, experts_all * capacity)
    placing = jnp.any(slot_index[None, :, :] == slot_iota[:, None, None], axis=2).astype(
        jnp.bfloat16
    )
    outgoing = jnp.dot(placing, normed, preferred_element_type=jnp.float32).astype(jnp.bfloat16)
    outgoing = outgoing.reshape(groups, local_experts, capacity, model_width)
    input_maps = expert_in.reshape(local_experts, model_width, -1)
    gate_up = jnp.einsum(
        "geci,eif->gecf",
        lax.all_to_all(outgoing, ("req", "exp"), split_axis=0, concat_axis=0, tiled=True),
        input_maps,
        preferred_element_type=jnp.float32,
    )
    half_units = gate_up.shape[-1] // 2
    activated = (jax.nn.silu(gate_up[..., :half_units]) * gate_up[..., half_units:]).astype(
        jnp.bfloat16
    )
    partial_value = jnp.einsum(
        "gecf,efi->geci", activated, expert_out, preferred_element_type=jnp.float32
    )
    half_width = model_width // lax.axis_size("head")
    head_start = lax.axis_index("head") * half_width
    returned_parts = lax.all_to_all(
        partial_value, ("req", "exp"), split_axis=0, concat_axis=0, tiled=True
    )
    both_halves = lax.psum(returned_parts, "head")
    returned = lax.dynamic_slice_in_dim(both_halves, head_start, half_width, 3).astype(jnp.bfloat16)
    flat_results = returned.reshape(experts_all * capacity, half_width)
    picked = jnp.take(flat_results, slot_index, axis=0).astype(jnp.float32)
    mixture = jnp.sum(picked * route_weights[:, :, None], axis=1)
    kept_hidden = lax.dynamic_slice_in_dim(hidden, head_start, half_width, 1)
    return (kept_hidden + mixture).astype(jnp.bfloat16)


def solution(mesh):
    return jax.shard_map(
        local,
        mesh=mesh,
        in_specs=(
            P("req", "exp", "head", None),
            P("req", "exp", "head", None),
            P("req", "exp", "head", None),
            P("req", "exp", "head", None),
            P("req", "exp", "head", None),
            P("req"),
            P(("req", "exp"), None),
            P("head", "exp"),
            P(),
            P(("req", "exp"), None),
            P(("req", "exp"), None),
            P(("req", "exp"), None, None, "head"),
            P(("req", "exp"), "head", None),
        ),
        out_specs=P(("req", "exp"), "head"),
        check_vma=False,
    )
```

```python
import functools
import math

import jax
import jax.numpy as jnp
from jax import lax
from jax.experimental import pallas as pl
from jax.experimental.pallas import tpu as pltpu
from jax.sharding import PartitionSpec as P

masked_score = -1e30
norm_epsilon = 1e-06
MESH = pl.DeviceIdType.MESH
BF = jnp.bfloat16
F32 = jnp.float32
PLANE = 16
DEPTH = 8
TILE = 256
TURN = 128
VMEM_LIMIT = 60 * 1024 * 1024


def place():
    return lax.axis_index("req"), lax.axis_index("head"), lax.axis_index("exp")


def remote(src, dst, send_sem, recv_sem, target):
    return pltpu.make_async_remote_copy(
        src_ref=src,
        dst_ref=dst,
        send_sem=send_sem,
        recv_sem=recv_sem,
        device_id=target,
        device_id_type=MESH,
    )


def rows16(index):
    return pl.ds(pl.multiple_of(index * 16, 16), 16)


def layer_kernel(
    span,
    q_ref,
    nk_ref,
    nv_ref,
    k_hbm,
    v_hbm,
    len_ref,
    res_ref,
    w_hbm,
    gain_ref,
    ids_ref,
    wts_ref,
    in_hbm,
    down_hbm,
    out_ref,
    raw,
    loose,
    k_ref,
    v_ref,
    bias,
    qbuf,
    scores_a,
    scores_b,
    probs_a,
    probs_b,
    stage,
    recv,
    split,
    flat,
    abuf,
    w_ref,
    pstage,
    pbuf,
    hid_ref,
    sq_stage,
    sq_recv,
    norm_ref,
    in_raw,
    in_ref,
    down_ref,
    meta_ref,
    zbuf,
    mbuf,
    xstage,
    xbuf,
    ystage,
    ybuf,
    rstage,
    rbuf,
    cstage,
    cbuf,
    kv_sems,
    w_sems,
    q_send,
    q_recv,
    f_send,
    f_recv,
    s_send,
    s_recv,
    a_send,
    a_recv,
    b_send,
    b_recv,
    p_send,
    p_recv,
    sq_sems,
    z_send,
    z_recv,
    m_send,
    m_recv,
    x_send,
    x_recv,
    h_send,
    h_recv,
    y_sems,
    r_send,
    r_recv,
    c_send,
    c_recv,
):
    z, c, me = place()
    other = 1 - c
    row_x = lax.div(me, 4)
    row_y = lax.rem(me, 4)

    def kv_copy(which, request):
        source = (k_hbm, v_hbm)[which]
        return pltpu.make_async_copy(
            source.at[request], raw.at[which, request], kv_sems.at[which, request]
        )

    def w_copy(which):
        source, target = ((w_hbm, w_ref), (in_hbm, in_raw), (down_hbm, down_ref))[which]
        return pltpu.make_async_copy(source, target, w_sems.at[which])

    @pl.loop(0, 4)
    def _(i):
        request = lax.rem(row_y + i, 4)
        kv_copy(0, request).start()
        kv_copy(1, request).start()

    for which in range(3):
        w_copy(which).start()

    barrier = pltpu.get_barrier_semaphore()

    def greet(*target):
        pl.semaphore_signal(barrier, inc=1, device_id=target, device_id_type=MESH)

    @pl.loop(1, PLANE)
    def _(i):
        peer = lax.rem(me + i, PLANE)
        greet(z, c, peer)
        greet(z, other, peer)

    @pl.loop(1, DEPTH)
    def _(i):
        greet(lax.rem(z + i, DEPTH), c, me)

    greet(z, other, me)
    meta_ref[...] = jnp.zeros((16, 128), F32)
    meta_ref[0:8, 0:16] = ids_ref[...].astype(F32)
    meta_ref[8:16, 0:16] = wts_ref[...]
    meta_ref[...] = pltpu.roll(meta_ref[...], 16 * z, 1)
    pl.semaphore_wait(barrier, 2 * PLANE - 1 + DEPTH - 1)

    def q_copy(source, target):
        return remote(
            q_ref,
            qbuf.at[:, pl.ds(pl.multiple_of((row_x * 4 + source) * 64, 64), 64), :],
            q_send.at[target],
            q_recv.at[source],
            (z, c, row_x * 4 + target),
        )

    @pl.loop(1, 4)
    def _(i):
        q_copy(row_y, lax.rem(row_y + i, 4)).start()

    def m_copy(source, target):
        return remote(
            meta_ref, mbuf.at[source], m_send.at[target], m_recv.at[source], (target, c, me)
        )

    @pl.loop(1, DEPTH)
    def _(i):
        m_copy(z, lax.rem(z + i, DEPTH)).start()

    mbuf[z] = meta_ref[...]
    qbuf[:, pl.ds(pl.multiple_of(me * 64, 64), 64), :] = q_ref[...]

    def f_copy(source, target):
        rows = pl.ds(pl.multiple_of(source * 256, 256), 256)
        return remote(
            qbuf.at[:, rows, :],
            qbuf.at[:, rows, :],
            f_send.at[target],
            f_recv.at[source],
            (z, c, target * 4 + row_y),
        )

    keys = span + 128
    key_iota = lax.broadcasted_iota(jnp.int32, (8, keys), 1)

    def arrange(request):
        cached = jnp.logical_and(key_iota < span, key_iota + me * span < len_ref[request])
        fresh = jnp.logical_and(key_iota >= span, key_iota < span + 4)
        bias[request] = jnp.where(jnp.logical_or(cached, fresh), 0.0, masked_score)
        for which in range(2):
            target = (k_ref, v_ref)[which]
            new = (nk_ref, nv_ref)[which]
            kv_copy(which, request).wait()

            @pl.loop(0, span // TILE)
            def _(i):
                rows = pl.ds(pl.multiple_of(i * 2 * TILE, 2 * TILE), 2 * TILE)
                loose[...] = raw[which, request, rows, :].astype(F32)
                into = pl.ds(pl.multiple_of(i * TILE, TILE), TILE)
                target[request, into, 0:128] = loose[pl.ds(0, TILE, 2), :].astype(BF)
                target[request, into, 128:256] = loose[pl.ds(1, TILE, 2), :].astype(BF)

            loose[0:8, :] = new[request].astype(F32)
            loose[8:256, :] = jnp.zeros((248, 128), F32)
            tail = pl.ds(span, 128)
            target[request, tail, 0:128] = loose[pl.ds(0, 128, 2), :].astype(BF)
            target[request, tail, 128:256] = loose[pl.ds(1, 128, 2), :].astype(BF)

    arrange(row_y)

    @pl.loop(1, 4)
    def _(i):
        q_copy(lax.rem(row_y + i, 4), row_y).wait_recv()

    f_copy(row_x, lax.rem(row_x + 3, 4)).start()
    f_copy(row_x, lax.rem(row_x + 1, 4)).start()

    row_iota = lax.broadcasted_iota(jnp.int32, (256, 128), 0)
    low = lax.rem(row_iota, 16) < 8
    low_mask = jnp.where(low, 1.0, 0.0).astype(BF)
    high_mask = jnp.where(low, 0.0, 1.0).astype(BF)
    stat_iota = lax.broadcasted_iota(jnp.int32, (16, 128), 0)
    factor = (128.0 ** -0.5) * math.log2(math.e)
    tiles = [slice(t * 128, t * 128 + 128) for t in range(keys // 128)]

    def s_copy(owner, source):
        return remote(
            stage.at[owner],
            recv.at[source],
            s_send.at[owner],
            s_recv.at[source],
            (z, c, owner),
        )

    def score(request, group, scores):
        q = qbuf[request, pl.ds(pl.multiple_of(group * 256, 256), 256), :]
        both = jnp.concatenate([q * low_mask, q * high_mask], axis=1)
        scores[...] = lax.dot_general(
            both, k_ref[request], (((1,), (1,)), ((), ())), preferred_element_type=F32
        )

    def soften(request, scores, probs):
        levels, totals = [], []
        for part in range(2):
            rows = slice(part * 128, part * 128 + 128)
            top = scores[rows, tiles[0]] + bias[request, 0:1, tiles[0]]
            for tile in tiles[1:]:
                top = jnp.maximum(top, scores[rows, tile] + bias[request, 0:1, tile])
            shift = jnp.max(top, axis=1, keepdims=True) * factor
            total = jnp.zeros((128, 128), F32)
            for tile in tiles:
                shown = scores[rows, tile] + bias[request, 0:1, tile]
                prob = jnp.exp2(shown * factor - shift)
                total = total + prob
                probs[rows, tile] = prob.astype(BF)
            total = jnp.sum(total, axis=1, keepdims=True)
            levels.append(shift + jnp.log2(total))
            totals.append(total)
        return jnp.concatenate(levels, axis=0), jnp.concatenate(totals, axis=0)

    def finish(owner, request, probs, level, total):
        sums = jnp.dot(probs[...], v_ref[request], preferred_element_type=F32)
        mean = jnp.where(low, sums[:, :128], sums[:, 128:]) / total
        turned = jnp.transpose(jnp.broadcast_to(level, (256, 128)))[0:1, :]
        stats = jnp.zeros((16, 128), F32)
        for half in range(2):
            rest = turned[:, half * 128 : half * 128 + 128]
            for term in range(3):
                part = rest.astype(BF).astype(F32)
                rest = rest - part
                stats = jnp.where(stat_iota == 2 * term + half, part, stats)
        stage[owner, 0:256, :] = mean.astype(BF)
        stage[owner, 256:272, :] = stats.astype(BF)

        @pl.when(owner != me)
        def _():
            s_copy(owner, me).start()

    @pl.loop(0, PLANE // 2)
    def _(i):
        group = lax.rem(row_x + lax.div(i, 2), 4)
        first = lax.rem(row_y + 2 * lax.rem(i, 2), 4)
        second = lax.rem(first + 1, 4)

        @pl.when(jnp.logical_and(i < 2, i > 0))
        def _():
            arrange(first)

        @pl.when(i < 2)
        def _():
            arrange(second)

        @pl.when(i == 1)
        def _():
            f_copy(row_x, lax.rem(row_x + 2, 4)).start()

        @pl.when(jnp.logical_and(i > 0, lax.rem(i, 2) == 0))
        def _():
            f_copy(group, row_x).wait_recv()

        score(first, group, scores_a)
        score(second, group, scores_b)
        level_a, total_a = soften(first, scores_a, probs_a)
        finish(first * 4 + group, first, probs_a, level_a, total_a)
        level_b, total_b = soften(second, scores_b, probs_b)
        finish(second * 4 + group, second, probs_b, level_b, total_b)

    recv[me] = stage[me]

    @pl.loop(1, PLANE)
    def _(i):
        s_copy(me, lax.rem(me + i, PLANE)).wait_recv()

    terms = recv[:, 256:272, :].astype(F32)
    term_iota = lax.broadcasted_iota(jnp.int32, (16, 16, 128), 1)
    columns = []
    for half in range(2):
        mine = jnp.logical_and(term_iota < 6, lax.rem(term_iota, 2) == half)
        level = jnp.sum(jnp.where(mine, terms, 0.0), axis=1)
        weight = jnp.exp2(level - jnp.max(level, axis=0, keepdims=True))
        weight = weight / jnp.sum(weight, axis=0, keepdims=True)
        padded = jnp.concatenate([weight, jnp.zeros((112, 128), F32)], axis=0)
        columns.append(jnp.transpose(padded))
    weights = jnp.concatenate(columns, axis=0)
    merged = jnp.zeros((256, 128), F32)
    for source in range(PLANE):
        merged = merged + weights[:, source : source + 1] * recv[source, 0:256, :].astype(F32)
    split[...] = merged.reshape(16, 16, 128)
    for head in range(16):
        flat[:, head * 128 : head * 128 + 128] = split[:, head, :].astype(BF)

    left, right = pl.ds(0, 1024), pl.ds(1024, 1024)

    def a_copy(axis, source, target):
        if axis == 0:
            spot, cols, device = (source, row_y), left, (z, c, target * 4 + row_y)
        else:
            spot, cols, device = (row_x, source), right, (z, c, row_x * 4 + target)
        return remote(
            flat.at[:, cols],
            abuf.at[spot[0], spot[1], :, cols],
            a_send.at[axis, target],
            a_recv.at[axis, source],
            device,
        )

    def b_copy(axis, source, target):
        if axis == 0:
            block, device = abuf.at[:, source, :, left], (z, c, row_x * 4 + target)
        else:
            block, device = abuf.at[source, :, :, right], (z, c, target * 4 + row_y)
        return remote(block, block, b_send.at[axis, target], b_recv.at[axis, source], device)

    @pl.loop(1, 4)
    def _(i):
        a_copy(0, row_x, lax.rem(row_x + i, 4)).start()
        a_copy(1, row_y, lax.rem(row_y + i, 4)).start()

    abuf[row_x, row_y] = flat[...]

    @pl.loop(1, DEPTH)
    def _(i):
        m_copy(lax.rem(z + i, DEPTH), z).wait_recv()

    @pl.loop(1, 4)
    def _(i):
        a_copy(0, lax.rem(row_x + i, 4), row_x).wait_recv()

    @pl.loop(1, 4)
    def _(i):
        b_copy(0, row_y, lax.rem(row_y + i, 4)).start()

    @pl.loop(1, 4)
    def _(i):
        a_copy(1, lax.rem(row_y + i, 4), row_y).wait_recv()

    @pl.loop(1, 4)
    def _(i):
        b_copy(1, row_x, lax.rem(row_x + i, 4)).start()

    meta = jnp.sum(mbuf[...], axis=0)
    expert_iota = lax.broadcasted_iota(jnp.int32, (16, 128), 0).astype(F32)
    expert_iota = expert_iota + (z * PLANE).astype(F32)
    named = jnp.zeros((16, 128), F32)
    weight = jnp.zeros((16, 128), F32)
    for k in range(8):
        hit = meta[k : k + 1, :] == expert_iota
        named = named + jnp.where(hit, 1.0, 0.0)
        weight = weight + jnp.where(hit, meta[8 + k : 9 + k, :], 0.0)
    from_row = lax.broadcasted_iota(jnp.int32, (128, 128), 0)
    to_row = lax.broadcasted_iota(jnp.int32, (128, 128), 1)
    same = lax.div(from_row, 16) == lax.div(to_row, 16)
    earlier = jnp.where(jnp.logical_and(same, from_row < to_row), 1.0, 0.0).astype(BF)
    rank = jnp.dot(named.astype(BF), earlier, preferred_element_type=F32)
    slot = 2.0 * lax.div(lax.broadcasted_iota(jnp.int32, (16, 128), 1), 16).astype(F32) + rank
    slot = jnp.where(named > 0.5, slot, -1.0)
    slot_iota = lax.broadcasted_iota(jnp.int32, (16, 16, 128), 1).astype(F32)
    chosen = slot[:, None, :] == slot_iota
    placing = jnp.where(chosen, 1.0, 0.0).reshape(256, 128).astype(BF)
    scaled = jnp.where(chosen, weight[:, None, :], 0.0).reshape(256, 128)
    turned = jnp.transpose(scaled)
    turned_high = turned.astype(BF)
    turned_low = (turned - turned_high.astype(F32)).astype(BF)

    w_copy(0).wait()

    @pl.loop(1, 4)
    def _(i):
        b_copy(0, lax.rem(row_y + i, 4), row_y).wait_recv()
        b_copy(1, lax.rem(row_x + i, 4), row_x).wait_recv()

    projected = jnp.dot(abuf[...].reshape(256, 2048), w_ref[...], preferred_element_type=F32)
    pstage[...] = projected.reshape(16, 16, 128)
    own_side = lax.div(me, 8)

    def p_copy(source_core, source, target):
        return remote(
            pstage.at[target],
            pbuf.at[source_core, lax.rem(source, 8)],
            p_send.at[target],
            p_recv.at[source_core, lax.rem(source, 8)],
            (z, lax.div(source, 8), target),
        )

    @pl.loop(1, PLANE)
    def _(i):
        p_copy(c, me, lax.rem(me + i, PLANE)).start()

    @pl.when(own_side != c)
    def _():
        p_copy(c, me, me).start()

    @pl.when(own_side == c)
    def _():
        pbuf[c, lax.rem(me, 8)] = pstage[me]

    @pl.loop(0, 8)
    def _(i):
        p_copy(other, c * 8 + i, me).wait_recv()

        @pl.when(c * 8 + i != me)
        def _():
            p_copy(c, c * 8 + i, me).wait_recv()

    mine = pl.ds(pl.multiple_of(c * 1024, 1024), 1024)
    theirs = pl.ds(pl.multiple_of(other * 1024, 1024), 1024)
    square = jnp.zeros((16, 128), F32)
    for part in range(8):
        cols = pl.ds(pl.multiple_of(c * 1024 + part * 128, 128), 128)
        hidden = res_ref[:, cols].astype(F32) + (pbuf[0, part] + pbuf[1, part])
        hid_ref[:, part * 128 : part * 128 + 128] = hidden
        square = square + hidden * hidden
    sq_stage[...] = square
    sq_copy = remote(sq_stage, sq_recv, sq_sems.at[0], sq_sems.at[1], (z, other, me))
    sq_copy.start()
    scaled_hidden = hid_ref[...] * gain_ref[:, mine]
    sq_copy.wait_recv()
    square = square + sq_recv[...]
    mean_square = jnp.sum(square, axis=1, keepdims=True) * (1.0 / 2048.0)
    norm_ref[...] = (scaled_hidden * lax.rsqrt(mean_square + norm_epsilon)).astype(BF)

    def z_copy(source, target):
        return remote(
            norm_ref, zbuf.at[rows16(source), :], z_send.at[target], z_recv.at[source], (target, c, me)
        )

    @pl.loop(1, DEPTH)
    def _(i):
        z_copy(z, lax.rem(z + i, DEPTH)).start()

    zbuf[rows16(z), :] = norm_ref[...]
    w_copy(1).wait()

    @pl.loop(0, 2048 // TURN)
    def _(i):
        rows = pl.ds(pl.multiple_of(i * TURN, TURN), TURN)
        for side in range(2):
            in_ref[rows, side * 384 : side * 384 + 384] = in_raw[rows, side, :]

    w_copy(2).wait()

    @pl.loop(1, DEPTH)
    def _(i):
        z_copy(lax.rem(z + i, DEPTH), z).wait_recv()

    xstage[...] = jnp.dot(placing, zbuf[...], preferred_element_type=F32).astype(BF)

    def x_copy(source, target):
        return remote(
            xstage.at[rows16(target), :],
            xbuf.at[rows16(source), mine],
            x_send.at[target],
            x_recv.at[source],
            (z, c, target),
        )

    def h_copy(source, columns):
        return remote(
            xbuf.at[rows16(source), columns],
            xbuf.at[rows16(source), columns],
            h_send.at[source],
            h_recv.at[source],
            (z, other, me),
        )

    @pl.loop(1, PLANE)
    def _(i):
        x_copy(me, lax.rem(me + i, PLANE)).start()

    xbuf[rows16(me), mine] = xstage[rows16(me), :]
    h_copy(me, mine).start()

    @pl.loop(1, PLANE)
    def _(i):
        peer = lax.rem(me + PLANE - i, PLANE)
        x_copy(peer, me).wait_recv()
        h_copy(peer, mine).start()

    @pl.loop(0, PLANE)
    def _(i):
        h_copy(i, theirs).wait_recv()

    gate_up = jnp.dot(xbuf[...], in_ref[...], preferred_element_type=F32)
    gate = gate_up[:, :384]
    active = (gate / (1.0 + jnp.exp(-gate)) * gate_up[:, 384:]).astype(BF)
    ystage[...] = jnp.dot(active, down_ref[:, theirs], preferred_element_type=F32).astype(BF)
    y_copy = remote(ystage, ybuf, y_sems.at[0], y_sems.at[1], (z, other, me))
    y_copy.start()
    own = jnp.dot(active, down_ref[:, mine], preferred_element_type=F32)
    y_copy.wait_recv()
    rstage[...] = (own + ybuf[...].astype(F32)).astype(BF)

    def r_copy(source, target):
        return remote(
            rstage.at[rows16(target), :],
            rbuf.at[rows16(source), :],
            r_send.at[target],
            r_recv.at[source],
            (z, c, target),
        )

    @pl.loop(1, PLANE)
    def _(i):
        r_copy(me, lax.rem(me + i, PLANE)).start()

    rbuf[rows16(me), :] = rstage[rows16(me), :]

    @pl.loop(1, PLANE)
    def _(i):
        r_copy(lax.rem(me + i, PLANE), me).wait_recv()

    mixed = jnp.dot(turned_high, rbuf[...], preferred_element_type=F32)
    mixed = mixed + jnp.dot(turned_low, rbuf[...], preferred_element_type=F32)
    cstage[...] = mixed.astype(BF)

    def c_copy(source, target):
        return remote(
            cstage.at[rows16(target), :],
            cbuf.at[source],
            c_send.at[target],
            c_recv.at[source],
            (target, c, me),
        )

    @pl.loop(1, DEPTH)
    def _(i):
        c_copy(z, lax.rem(z + i, DEPTH)).start()

    cbuf[z] = cstage[rows16(z), :]

    @pl.loop(1, DEPTH)
    def _(i):
        c_copy(lax.rem(z + i, DEPTH), z).wait_recv()

    total = hid_ref[...]
    for source in range(DEPTH):
        total = total + cbuf[source].astype(F32)
    out_ref[...] = total.astype(BF)

    @pl.loop(1, 4)
    def _(i):
        side_x, side_y = lax.rem(row_x + i, 4), lax.rem(row_y + i, 4)
        q_copy(row_y, side_y).wait_send()
        f_copy(row_x, side_x).wait_send()
        a_copy(0, row_x, side_x).wait_send()
        a_copy(1, row_y, side_y).wait_send()
        b_copy(0, row_y, side_y).wait_send()
        b_copy(1, row_x, side_x).wait_send()

    @pl.loop(1, PLANE)
    def _(i):
        peer = lax.rem(me + i, PLANE)
        s_copy(peer, me).wait_send()
        p_copy(c, me, peer).wait_send()
        x_copy(me, peer).wait_send()
        r_copy(me, peer).wait_send()

    @pl.when(own_side != c)
    def _():
        p_copy(c, me, me).wait_send()

    @pl.loop(0, PLANE)
    def _(i):
        h_copy(i, mine).wait_send()

    sq_copy.wait_send()
    y_copy.wait_send()

    @pl.loop(1, DEPTH)
    def _(i):
        peer = lax.rem(z + i, DEPTH)
        m_copy(z, peer).wait_send()
        z_copy(z, peer).wait_send()
        c_copy(z, peer).wait_send()


def dma(*shape):
    return pltpu.SemaphoreType.DMA(shape)


def layer(span, *operands):
    specs = [pl.BlockSpec(memory_space=pltpu.VMEM)] * 13
    for held in (3, 4, 7, 11, 12):
        specs[held] = pl.BlockSpec(memory_space=pl.ANY)
    specs[5] = pl.BlockSpec(memory_space=pltpu.SMEM)
    keys = span + 128
    return pl.pallas_call(
        functools.partial(layer_kernel, span),
        out_shape=jax.ShapeDtypeStruct((16, 1024), BF),
        in_specs=specs,
        out_specs=pl.BlockSpec(memory_space=pltpu.VMEM),
        scratch_shapes=[
            pltpu.VMEM((2, 4, 2 * span, 128), BF),
            pltpu.VMEM((2 * TILE, 128), F32),
            pltpu.VMEM((4, keys, 256), BF),
            pltpu.VMEM((4, keys, 256), BF),
            pltpu.VMEM((4, 8, keys), F32),
            pltpu.VMEM((4, 1024, 128), BF),
            pltpu.VMEM((256, keys), F32),
            pltpu.VMEM((256, keys), F32),
            pltpu.VMEM((256, keys), BF),
            pltpu.VMEM((256, keys), BF),
            pltpu.VMEM((PLANE, 272, 128), BF),
            pltpu.VMEM((PLANE, 272, 128), BF),
            pltpu.VMEM((16, 16, 128), F32),
            pltpu.VMEM((16, 2048), BF),
            pltpu.VMEM((4, 4, 16, 2048), BF),
            pltpu.VMEM((2048, 128), BF),
            pltpu.VMEM((16, 16, 128), F32),
            pltpu.VMEM((2, 8, 16, 128), F32),
            pltpu.VMEM((16, 1024), F32),
            pltpu.VMEM((16, 128), F32),
            pltpu.VMEM((16, 128), F32),
            pltpu.VMEM((16, 1024), BF),
            pltpu.VMEM((2048, 2, 384), BF),
            pltpu.VMEM((2048, 768), BF),
            pltpu.VMEM((384, 2048), BF),
            pltpu.VMEM((16, 128), F32),
            pltpu.VMEM((128, 1024), BF),
            pltpu.VMEM((DEPTH, 16, 128), F32),
            pltpu.VMEM((256, 1024), BF),
            pltpu.VMEM((256, 2048), BF),
            pltpu.VMEM((256, 1024), BF),
            pltpu.VMEM((256, 1024), BF),
            pltpu.VMEM((256, 1024), BF),
            pltpu.VMEM((256, 1024), BF),
            pltpu.VMEM((128, 1024), BF),
            pltpu.VMEM((DEPTH, 16, 1024), BF),
            dma(2, 4),
            dma(3),
            dma(4),
            dma(4),
            dma(4),
            dma(4),
            dma(PLANE),
            dma(PLANE),
            dma(2, 4),
            dma(2, 4),
            dma(2, 4),
            dma(2, 4),
            dma(PLANE),
            dma(2, 8),
            dma(2),
            dma(DEPTH),
            dma(DEPTH),
            dma(DEPTH),
            dma(DEPTH),
            dma(PLANE),
            dma(PLANE),
            dma(PLANE),
            dma(PLANE),
            dma(2),
            dma(PLANE),
            dma(PLANE),
            dma(DEPTH),
            dma(DEPTH),
        ],
        compiler_params=pltpu.CompilerParams(
            collective_id=0, has_side_effects=True, vmem_limit_bytes=VMEM_LIMIT
        ),
    )(*operands)


def local(
    queries,
    new_keys,
    new_values,
    key_cache,
    value_cache,
    lengths,
    residual,
    out_weight,
    norm_gain,
    route_ids,
    route_weights,
    expert_in,
    expert_out,
):
    requests, span = key_cache.shape[:2]
    return layer(
        span,
        queries.reshape(requests, 64, 128),
        new_keys.reshape(requests, 8, 128),
        new_values.reshape(requests, 8, 128),
        key_cache.reshape(requests, 2 * span, 128),
        value_cache.reshape(requests, 2 * span, 128),
        lengths,
        residual,
        out_weight,
        norm_gain.reshape(1, -1),
        route_ids.T,
        route_weights.T,
        expert_in.reshape(2048, 2, 384),
        expert_out.reshape(384, 2048),
    )


def solution(mesh):
    return jax.shard_map(
        local,
        mesh=mesh,
        in_specs=(
            P("req", "exp", "head", None),
            P("req", "exp", "head", None),
            P("req", "exp", "head", None),
            P("req", "exp", "head", None),
            P("req", "exp", "head", None),
            P("req"),
            P(("req", "exp"), None),
            P("head", "exp"),
            P(),
            P(("req", "exp"), None),
            P(("req", "exp"), None),
            P(("req", "exp"), None, None, "head"),
            P(("req", "exp"), "head", None),
        ),
        out_specs=P(("req", "exp"), "head"),
        check_vma=False,
    )
```

```python
import functools
import math

import jax
import jax.numpy as jnp
from jax import lax
from jax.experimental import pallas as pl
from jax.experimental.pallas import tpu as pltpu
from jax.sharding import PartitionSpec as P

masked_score = -1e30
norm_epsilon = 1e-06
MESH = pl.DeviceIdType.MESH
BF = jnp.bfloat16
F32 = jnp.float32
PLANE = 16
DEPTH = 8
TILE = 256
TURN = 128
VMEM_LIMIT = 60 * 1024 * 1024


def place():
    return lax.axis_index("req"), lax.axis_index("head"), lax.axis_index("exp")


def remote(src, dst, send_sem, recv_sem, target):
    return pltpu.make_async_remote_copy(
        src_ref=src,
        dst_ref=dst,
        send_sem=send_sem,
        recv_sem=recv_sem,
        device_id=target,
        device_id_type=MESH,
    )


def rows16(index):
    return pl.ds(pl.multiple_of(index * 16, 16), 16)


def layer_kernel(
    span,
    q_ref,
    nk_ref,
    nv_ref,
    k_hbm,
    v_hbm,
    len_ref,
    res_ref,
    w_hbm,
    gain_ref,
    ids_ref,
    wts_ref,
    in_hbm,
    down_hbm,
    out_ref,
    raw,
    loose,
    k_ref,
    v_ref,
    bias,
    qbuf,
    scores_a,
    scores_b,
    probs_a,
    probs_b,
    stage,
    recv,
    split,
    flat,
    abuf,
    w_ref,
    pstage,
    pbuf,
    hid_ref,
    sq_stage,
    sq_recv,
    norm_ref,
    in_raw,
    in_ref,
    down_ref,
    meta_ref,
    zbuf,
    mbuf,
    xstage,
    xbuf,
    own_ref,
    ystage,
    ybuf,
    rstage,
    rbuf,
    cstage,
    cbuf,
    kv_sems,
    w_sems,
    q_send,
    q_recv,
    f_send,
    f_recv,
    s_send,
    s_recv,
    a_send,
    a_recv,
    b_send,
    b_recv,
    p_send,
    p_recv,
    sq_sems,
    z_send,
    z_recv,
    m_send,
    m_recv,
    x_send,
    x_recv,
    h_send,
    h_recv,
    y_send,
    y_recv,
    r_send,
    r_recv,
    c_send,
    c_recv,
):
    after = []
    z, c, me = place()
    other = 1 - c
    row_x = lax.div(me, 4)
    row_y = lax.rem(me, 4)

    sign = 1 - 2 * lax.rem(row_x + row_y, 2)

    def moved(way, step_x, step_y):
        return lax.rem(row_x + way * step_x + 4, 4), lax.rem(row_y + way * step_y + 4, 4)

    def steps(k):
        step_x = lax.rem(k, 4)
        return step_x, lax.rem(step_x + lax.div(k, 4), 4)

    def partner(k):
        to_x, to_y = moved(sign, *steps(k))
        return to_x * 4 + to_y

    def origin(k):
        step_x, step_y = steps(k)
        from_x, from_y = moved(sign * (2 * lax.rem(step_x + step_y, 2) - 1), step_x, step_y)
        return from_x * 4 + from_y

    def kv_copy(which, request):
        source = (k_hbm, v_hbm)[which]
        return pltpu.make_async_copy(
            source.at[request], raw.at[which, request], kv_sems.at[which, request]
        )

    def w_copy(which):
        source, target = ((w_hbm, w_ref), (in_hbm, in_raw), (down_hbm, down_ref))[which]
        return pltpu.make_async_copy(source, target, w_sems.at[which])

    barrier = pltpu.get_barrier_semaphore()

    def greet(*target):
        pl.semaphore_signal(barrier, inc=1, device_id=target, device_id_type=MESH)

    @pl.loop(1, PLANE)
    def _(i):
        peer = lax.rem(me + i, PLANE)
        greet(z, c, peer)
        greet(z, other, peer)

    @pl.loop(1, DEPTH)
    def _(i):
        greet(lax.rem(z + i, DEPTH), c, me)

    greet(z, other, me)

    @pl.loop(0, 4)
    def _(i):
        request = lax.rem(2 + i, 4)
        kv_copy(0, request).start()
        kv_copy(1, request).start()

    for which in range(3):
        w_copy(which).start()

    meta_ref[...] = jnp.zeros((16, 128), F32)
    meta_ref[0:8, 0:16] = ids_ref[...].astype(F32)
    meta_ref[8:16, 0:16] = wts_ref[...]
    meta_ref[...] = pltpu.roll(meta_ref[...], 16 * z, 1)
    pl.semaphore_wait(barrier, 2 * PLANE - 1 + DEPTH - 1)

    def q_copy(axis, source, target):
        span_rows = pl.ds(2 * axis, 2)
        if axis == 0:
            block, device = (source, row_y), (z, c, target * 4 + row_y)
        else:
            block, device = (row_x, source), (z, c, row_x * 4 + target)
        cols = pl.ds(pl.multiple_of(block[1] * 64, 64), 64)
        return remote(
            q_ref.at[span_rows],
            qbuf.at[span_rows, block[0], cols, :],
            q_send.at[axis, target],
            q_recv.at[axis, source],
            device,
        )

    @pl.loop(1, 4)
    def _(i):
        q_copy(1, row_y, lax.rem(row_y + i, 4)).start()
        q_copy(0, row_x, lax.rem(row_x + i, 4)).start()

    @after.append
    def _():
        @pl.loop(1, 4)
        def _(i):
            q_copy(0, row_x, lax.rem(row_x + i, 4)).wait_send()
            q_copy(1, row_y, lax.rem(row_y + i, 4)).wait_send()

    def m_copy(source, target):
        return remote(
            meta_ref, mbuf.at[source], m_send.at[target], m_recv.at[source], (target, c, me)
        )

    @pl.loop(1, DEPTH)
    def _(i):
        m_copy(z, lax.rem(z + i, DEPTH)).start()

    @after.append
    def _():
        @pl.loop(1, DEPTH)
        def _(i):
            m_copy(z, lax.rem(z + i, DEPTH)).wait_send()

    mbuf[z] = meta_ref[...]
    qbuf[:, row_x, pl.ds(pl.multiple_of(row_y * 64, 64), 64), :] = q_ref[...]

    def f_copy(axis, source, target):
        if axis == 0:
            cols = pl.ds(pl.multiple_of(source * 64, 64), 64)
            block, device = qbuf.at[0:2, :, cols, :], (z, c, row_x * 4 + target)
        else:
            block, device = qbuf.at[2:4, source, :, :], (z, c, target * 4 + row_y)
        return remote(block, block, f_send.at[axis, target], f_recv.at[axis, source], device)

    keys = span + 128
    key_iota = lax.broadcasted_iota(jnp.int32, (8, keys), 1)

    def arrange(request):
        cached = jnp.logical_and(key_iota < span, key_iota + me * span < len_ref[request])
        fresh = jnp.logical_and(key_iota >= span, key_iota < span + 4)
        bias[request] = jnp.where(jnp.logical_or(cached, fresh), 0.0, masked_score)
        for which in range(2):
            target = (k_ref, v_ref)[which]
            new = (nk_ref, nv_ref)[which]
            kv_copy(which, request).wait()

            @pl.loop(0, span // TILE)
            def _(i):
                rows = pl.ds(pl.multiple_of(i * 2 * TILE, 2 * TILE), 2 * TILE)
                loose[...] = raw[which, request, rows, :].astype(F32)
                into = pl.ds(pl.multiple_of(i * TILE, TILE), TILE)
                target[request, into, 0:128] = loose[pl.ds(0, TILE, 2), :].astype(BF)
                target[request, into, 128:256] = loose[pl.ds(1, TILE, 2), :].astype(BF)

            loose[0:8, :] = new[request].astype(F32)
            loose[8:256, :] = jnp.zeros((248, 128), F32)
            tail = pl.ds(span, 128)
            target[request, tail, 0:128] = loose[pl.ds(0, 128, 2), :].astype(BF)
            target[request, tail, 128:256] = loose[pl.ds(1, 128, 2), :].astype(BF)

    arrange(2)

    @pl.loop(1, 4)
    def _(i):
        q_copy(1, lax.rem(row_y + i, 4), row_y).wait_recv()

    @pl.loop(1, 4)
    def _(i):
        f_copy(1, row_x, lax.rem(row_x + i, 4)).start()

    @pl.loop(1, 4)
    def _(i):
        q_copy(0, lax.rem(row_x + i, 4), row_x).wait_recv()

    @pl.loop(1, 4)
    def _(i):
        f_copy(0, row_y, lax.rem(row_y + i, 4)).start()

    @after.append
    def _():
        @pl.loop(1, 4)
        def _(i):
            f_copy(0, row_y, lax.rem(row_y + i, 4)).wait_send()
            f_copy(1, row_x, lax.rem(row_x + i, 4)).wait_send()

    arrange(3)
    arrange(0)
    arrange(1)

    @pl.loop(1, 4)
    def _(i):
        f_copy(1, lax.rem(row_x + i, 4), row_x).wait_recv()
        f_copy(0, lax.rem(row_y + i, 4), row_y).wait_recv()

    row_iota = lax.broadcasted_iota(jnp.int32, (256, 128), 0)
    low = lax.rem(row_iota, 16) < 8
    low_mask = jnp.where(low, 1.0, 0.0).astype(BF)
    high_mask = jnp.where(low, 0.0, 1.0).astype(BF)
    stat_iota = lax.broadcasted_iota(jnp.int32, (16, 128), 0)
    factor = (128.0 ** -0.5) * math.log2(math.e)
    tiles = [slice(t * 128, t * 128 + 128) for t in range(keys // 128)]

    def s_copy(owner, source):
        return remote(
            stage.at[owner],
            recv.at[source],
            s_send.at[owner],
            s_recv.at[source],
            (z, c, owner),
        )

    def score(request, group, scores):
        q = qbuf[request, group]
        both = jnp.concatenate([q * low_mask, q * high_mask], axis=1)
        scores[...] = lax.dot_general(
            both, k_ref[request], (((1,), (1,)), ((), ())), preferred_element_type=F32
        )

    def soften(request, scores, probs):
        levels, totals = [], []
        for part in range(2):
            rows = slice(part * 128, part * 128 + 128)
            top = scores[rows, tiles[0]] + bias[request, 0:1, tiles[0]]
            for tile in tiles[1:]:
                top = jnp.maximum(top, scores[rows, tile] + bias[request, 0:1, tile])
            shift = jnp.max(top, axis=1, keepdims=True) * factor
            total = jnp.zeros((128, 128), F32)
            for tile in tiles:
                shown = scores[rows, tile] + bias[request, 0:1, tile]
                prob = jnp.exp2(shown * factor - shift)
                total = total + prob
                probs[rows, tile] = prob.astype(BF)
            total = jnp.sum(total, axis=1, keepdims=True)
            levels.append(shift + jnp.log2(total))
            totals.append(total)
        return jnp.concatenate(levels, axis=0), jnp.concatenate(totals, axis=0)

    def finish(owner, request, probs, level, total):
        sums = jnp.dot(probs[...], v_ref[request], preferred_element_type=F32)
        mean = jnp.where(low, sums[:, :128], sums[:, 128:]) / total
        turned = jnp.transpose(jnp.broadcast_to(level, (256, 128)))[0:1, :]
        stats = jnp.zeros((16, 128), F32)
        for half in range(2):
            rest = turned[:, half * 128 : half * 128 + 128]
            for term in range(3):
                part = rest.astype(BF).astype(F32)
                rest = rest - part
                stats = jnp.where(stat_iota == 2 * term + half, part, stats)
        stage[owner, 0:256, :] = mean.astype(BF)
        stage[owner, 256:272, :] = stats.astype(BF)

        @pl.when(owner != me)
        def _():
            s_copy(owner, me).start()

    @after.append
    def _():
        @pl.loop(1, PLANE)
        def _(i):
            s_copy(lax.rem(me + i, PLANE), me).wait_send()

    @pl.loop(0, PLANE // 2)
    def _(i):
        step_x = lax.rem(lax.div(i, 2) + 1, 4)
        request, group_a = moved(sign, step_x, 2 + lax.rem(i, 2))
        group_b = moved(sign, step_x, 1 - lax.rem(i, 2))[1]
        score(request, group_a, scores_a)
        score(request, group_b, scores_b)
        level_a, total_a = soften(request, scores_a, probs_a)
        finish(request * 4 + group_a, request, probs_a, level_a, total_a)
        level_b, total_b = soften(request, scores_b, probs_b)
        finish(request * 4 + group_b, request, probs_b, level_b, total_b)

    recv[me] = stage[me]

    @pl.loop(1, PLANE)
    def _(i):
        s_copy(me, lax.rem(me + i, PLANE)).wait_recv()

    terms = recv[:, 256:272, :].astype(F32)
    term_iota = lax.broadcasted_iota(jnp.int32, (16, 16, 128), 1)
    columns = []
    for half in range(2):
        mine = jnp.logical_and(term_iota < 6, lax.rem(term_iota, 2) == half)
        level = jnp.sum(jnp.where(mine, terms, 0.0), axis=1)
        weight = jnp.exp2(level - jnp.max(level, axis=0, keepdims=True))
        weight = weight / jnp.sum(weight, axis=0, keepdims=True)
        padded = jnp.concatenate([weight, jnp.zeros((112, 128), F32)], axis=0)
        columns.append(jnp.transpose(padded))
    weights = jnp.concatenate(columns, axis=0)
    merged = jnp.zeros((256, 128), F32)
    for source in range(PLANE):
        merged = merged + weights[:, source : source + 1] * recv[source, 0:256, :].astype(F32)
    split[...] = merged.reshape(16, 16, 128)
    for head in range(16):
        flat[:, head * 128 : head * 128 + 128] = split[:, head, :].astype(BF)

    left, right = pl.ds(0, 1024), pl.ds(1024, 1024)

    def a_copy(axis, source, target):
        if axis == 0:
            spot, cols, device = (source, row_y), left, (z, c, target * 4 + row_y)
        else:
            spot, cols, device = (row_x, source), right, (z, c, row_x * 4 + target)
        return remote(
            flat.at[:, cols],
            abuf.at[spot[0], spot[1], :, cols],
            a_send.at[axis, target],
            a_recv.at[axis, source],
            device,
        )

    def b_copy(axis, source, target):
        if axis == 0:
            block, device = abuf.at[:, source, :, left], (z, c, row_x * 4 + target)
        else:
            block, device = abuf.at[source, :, :, right], (z, c, target * 4 + row_y)
        return remote(block, block, b_send.at[axis, target], b_recv.at[axis, source], device)

    @pl.loop(1, 4)
    def _(i):
        a_copy(0, row_x, lax.rem(row_x + i, 4)).start()
        a_copy(1, row_y, lax.rem(row_y + i, 4)).start()

    @after.append
    def _():
        @pl.loop(1, 4)
        def _(i):
            a_copy(0, row_x, lax.rem(row_x + i, 4)).wait_send()
            a_copy(1, row_y, lax.rem(row_y + i, 4)).wait_send()

    abuf[row_x, row_y] = flat[...]

    @pl.loop(1, DEPTH)
    def _(i):
        m_copy(lax.rem(z + i, DEPTH), z).wait_recv()

    @pl.loop(1, 4)
    def _(i):
        a_copy(0, lax.rem(row_x + i, 4), row_x).wait_recv()

    @pl.loop(1, 4)
    def _(i):
        b_copy(0, row_y, lax.rem(row_y + i, 4)).start()

    @pl.loop(1, 4)
    def _(i):
        a_copy(1, lax.rem(row_y + i, 4), row_y).wait_recv()

    @pl.loop(1, 4)
    def _(i):
        b_copy(1, row_x, lax.rem(row_x + i, 4)).start()

    @after.append
    def _():
        @pl.loop(1, 4)
        def _(i):
            b_copy(0, row_y, lax.rem(row_y + i, 4)).wait_send()
            b_copy(1, row_x, lax.rem(row_x + i, 4)).wait_send()

    meta = jnp.sum(mbuf[...], axis=0)
    expert_iota = lax.broadcasted_iota(jnp.int32, (16, 128), 0).astype(F32)
    expert_iota = expert_iota + (z * PLANE).astype(F32)
    named = jnp.zeros((16, 128), F32)
    weight = jnp.zeros((16, 128), F32)
    for k in range(8):
        hit = meta[k : k + 1, :] == expert_iota
        named = named + jnp.where(hit, 1.0, 0.0)
        weight = weight + jnp.where(hit, meta[8 + k : 9 + k, :], 0.0)
    from_row = lax.broadcasted_iota(jnp.int32, (128, 128), 0)
    to_row = lax.broadcasted_iota(jnp.int32, (128, 128), 1)
    same = lax.div(from_row, 16) == lax.div(to_row, 16)
    earlier = jnp.where(jnp.logical_and(same, from_row < to_row), 1.0, 0.0).astype(BF)
    rank = jnp.dot(named.astype(BF), earlier, preferred_element_type=F32)
    slot = 2.0 * lax.div(lax.broadcasted_iota(jnp.int32, (16, 128), 1), 16).astype(F32) + rank
    slot = jnp.where(named > 0.5, slot, -1.0)
    slot_iota = lax.broadcasted_iota(jnp.int32, (16, 16, 128), 1).astype(F32)
    chosen = slot[:, None, :] == slot_iota
    placing = jnp.where(chosen, 1.0, 0.0).reshape(256, 128).astype(BF)
    scaled = jnp.where(chosen, weight[:, None, :], 0.0).reshape(256, 128)
    turned = jnp.transpose(scaled)
    turned_high = turned.astype(BF)
    turned_low = (turned - turned_high.astype(F32)).astype(BF)

    w_copy(0).wait()

    @pl.loop(1, 4)
    def _(i):
        b_copy(0, lax.rem(row_y + i, 4), row_y).wait_recv()
        b_copy(1, lax.rem(row_x + i, 4), row_x).wait_recv()

    projected = jnp.dot(abuf[...].reshape(256, 2048), w_ref[...], preferred_element_type=F32)
    pstage[...] = projected.reshape(16, 16, 128)
    own_side = lax.div(me, 8)

    def p_copy(source_core, source, target):
        return remote(
            pstage.at[target],
            pbuf.at[source_core, lax.rem(source, 8)],
            p_send.at[target],
            p_recv.at[source_core, lax.rem(source, 8)],
            (z, lax.div(source, 8), target),
        )

    @pl.loop(1, PLANE)
    def _(i):
        p_copy(c, me, partner(i)).start()

    @pl.when(own_side != c)
    def _():
        p_copy(c, me, me).start()

    @after.append
    def _():
        @pl.loop(1, PLANE)
        def _(i):
            p_copy(c, me, lax.rem(me + i, PLANE)).wait_send()

    @after.append
    def _():
        @pl.when(own_side != c)
        def _():
            p_copy(c, me, me).wait_send()

    @pl.when(own_side == c)
    def _():
        pbuf[c, lax.rem(me, 8)] = pstage[me]

    @pl.loop(0, 8)
    def _(i):
        p_copy(other, c * 8 + i, me).wait_recv()

        @pl.when(c * 8 + i != me)
        def _():
            p_copy(c, c * 8 + i, me).wait_recv()

    mine = pl.ds(pl.multiple_of(c * 1024, 1024), 1024)
    theirs = pl.ds(pl.multiple_of(other * 1024, 1024), 1024)
    square = jnp.zeros((16, 128), F32)
    for part in range(8):
        cols = pl.ds(pl.multiple_of(c * 1024 + part * 128, 128), 128)
        hidden = res_ref[:, cols].astype(F32) + (pbuf[0, part] + pbuf[1, part])
        hid_ref[:, part * 128 : part * 128 + 128] = hidden
        square = square + hidden * hidden
    sq_stage[...] = square
    sq_copy = remote(sq_stage, sq_recv, sq_sems.at[0], sq_sems.at[1], (z, other, me))
    sq_copy.start()
    after.append(sq_copy.wait_send)
    scaled_hidden = hid_ref[...] * gain_ref[:, mine]
    sq_copy.wait_recv()
    square = square + sq_recv[...]
    mean_square = jnp.sum(square, axis=1, keepdims=True) * (1.0 / 2048.0)
    norm_ref[...] = (scaled_hidden * lax.rsqrt(mean_square + norm_epsilon)).astype(BF)

    def z_copy(source, target):
        return remote(
            norm_ref, zbuf.at[rows16(source), :], z_send.at[target], z_recv.at[source], (target, c, me)
        )

    @pl.loop(1, DEPTH)
    def _(i):
        z_copy(z, lax.rem(z + i, DEPTH)).start()

    @after.append
    def _():
        @pl.loop(1, DEPTH)
        def _(i):
            z_copy(z, lax.rem(z + i, DEPTH)).wait_send()

    zbuf[rows16(z), :] = norm_ref[...]
    w_copy(1).wait()

    @pl.loop(0, 2048 // TURN)
    def _(i):
        rows = pl.ds(pl.multiple_of(i * TURN, TURN), TURN)
        for side in range(2):
            in_ref[rows, side * 384 : side * 384 + 384] = in_raw[rows, side, :]

    w_copy(2).wait()

    @pl.loop(1, DEPTH)
    def _(i):
        z_copy(lax.rem(z + i, DEPTH), z).wait_recv()

    xstage[...] = jnp.dot(placing, zbuf[...], preferred_element_type=F32).astype(BF)

    def x_copy(step):
        target = partner(step)
        return remote(
            xstage.at[rows16(target), :],
            xbuf.at[rows16(step), mine],
            x_send.at[step],
            x_recv.at[step],
            (z, c, target),
        )

    def h_copy(step, columns):
        block = xbuf.at[rows16(step), columns]
        return remote(block, block, h_send.at[step], h_recv.at[step], (z, other, me))

    def y_copy(half):
        rows = pl.ds(half * 128, 128)
        return remote(
            ystage.at[rows, :], ybuf.at[rows, :], y_send.at[half], y_recv.at[half], (z, other, me)
        )

    def r_copy(step, expert):
        return remote(
            rstage.at[rows16(step), :],
            rbuf.at[rows16(expert), :],
            r_send.at[step],
            r_recv.at[step],
            (z, c, origin(step)),
        )

    def forward(start, stop):
        @pl.loop(start, stop)
        def _(i):
            x_copy(i).wait_recv()
            h_copy(i, mine).start()

    def evaluate(half):
        @pl.loop(8 * half, 8 * half + 8)
        def _(i):
            h_copy(i, theirs).wait_recv()

        rows = slice(128 * half, 128 * half + 128)
        gate_up = jnp.dot(xbuf[rows, :], in_ref[...], preferred_element_type=F32)
        gate = gate_up[:, :384]
        active = (gate / (1.0 + jnp.exp(-gate)) * gate_up[:, 384:]).astype(BF)
        partial = jnp.dot(active, down_ref[:, theirs], preferred_element_type=F32)
        ystage[rows, :] = partial.astype(BF)
        y_copy(half).start()
        own_ref[rows, :] = jnp.dot(active, down_ref[:, mine], preferred_element_type=F32)

    def give_back(half):
        rows = slice(128 * half, 128 * half + 128)
        y_copy(half).wait_recv()
        rstage[rows, :] = (own_ref[rows, :] + ybuf[rows, :].astype(F32)).astype(BF)

        @pl.loop(max(1, 8 * half), 8 * half + 8)
        def _(i):
            r_copy(i, me).start()

    @pl.loop(1, PLANE)
    def _(i):
        x_copy(i).start()

    @after.append
    def _():
        @pl.loop(1, PLANE)
        def _(i):
            x_copy(i).wait_send()

    @after.append
    def _():
        @pl.loop(0, PLANE)
        def _(i):
            h_copy(i, mine).wait_send()

    xbuf[0:16, mine] = xstage[rows16(me), :]
    h_copy(0, mine).start()
    forward(1, 8)
    evaluate(0)
    forward(8, PLANE)
    give_back(0)
    after.append(y_copy(0).wait_send)
    after.append(y_copy(1).wait_send)
    @after.append
    def _():
        @pl.loop(1, PLANE)
        def _(i):
            r_copy(i, me).wait_send()

    rbuf[rows16(me), :] = rstage[0:16, :]
    evaluate(1)
    give_back(1)

    @pl.loop(1, PLANE)
    def _(i):
        r_copy(i, partner(i)).wait_recv()

    mixed = jnp.dot(turned_high, rbuf[...], preferred_element_type=F32)
    mixed = mixed + jnp.dot(turned_low, rbuf[...], preferred_element_type=F32)
    cstage[...] = mixed.astype(BF)

    def c_copy(source, target):
        return remote(
            cstage.at[rows16(target), :],
            cbuf.at[source],
            c_send.at[target],
            c_recv.at[source],
            (target, c, me),
        )

    @pl.loop(1, DEPTH)
    def _(i):
        c_copy(z, lax.rem(z + i, DEPTH)).start()

    @after.append
    def _():
        @pl.loop(1, DEPTH)
        def _(i):
            c_copy(z, lax.rem(z + i, DEPTH)).wait_send()

    cbuf[z] = cstage[rows16(z), :]

    @pl.loop(1, DEPTH)
    def _(i):
        c_copy(lax.rem(z + i, DEPTH), z).wait_recv()

    total = hid_ref[...]
    for source in range(DEPTH):
        total = total + cbuf[source].astype(F32)
    out_ref[...] = total.astype(BF)

    for settle in after:
        settle()


def dma(*shape):
    return pltpu.SemaphoreType.DMA(shape)


def layer(span, *operands):
    specs = [pl.BlockSpec(memory_space=pltpu.VMEM)] * 13
    for held in (3, 4, 7, 11, 12):
        specs[held] = pl.BlockSpec(memory_space=pl.ANY)
    specs[5] = pl.BlockSpec(memory_space=pltpu.SMEM)
    keys = span + 128
    return pl.pallas_call(
        functools.partial(layer_kernel, span),
        out_shape=jax.ShapeDtypeStruct((16, 1024), BF),
        in_specs=specs,
        out_specs=pl.BlockSpec(memory_space=pltpu.VMEM),
        scratch_shapes=[
            pltpu.VMEM((2, 4, 2 * span, 128), BF),
            pltpu.VMEM((2 * TILE, 128), F32),
            pltpu.VMEM((4, keys, 256), BF),
            pltpu.VMEM((4, keys, 256), BF),
            pltpu.VMEM((4, 8, keys), F32),
            pltpu.VMEM((4, 4, 256, 128), BF),
            pltpu.VMEM((256, keys), F32),
            pltpu.VMEM((256, keys), F32),
            pltpu.VMEM((256, keys), BF),
            pltpu.VMEM((256, keys), BF),
            pltpu.VMEM((PLANE, 272, 128), BF),
            pltpu.VMEM((PLANE, 272, 128), BF),
            pltpu.VMEM((16, 16, 128), F32),
            pltpu.VMEM((16, 2048), BF),
            pltpu.VMEM((4, 4, 16, 2048), BF),
            pltpu.VMEM((2048, 128), BF),
            pltpu.VMEM((16, 16, 128), F32),
            pltpu.VMEM((2, 8, 16, 128), F32),
            pltpu.VMEM((16, 1024), F32),
            pltpu.VMEM((16, 128), F32),
            pltpu.VMEM((16, 128), F32),
            pltpu.VMEM((16, 1024), BF),
            pltpu.VMEM((2048, 2, 384), BF),
            pltpu.VMEM((2048, 768), BF),
            pltpu.VMEM((384, 2048), BF),
            pltpu.VMEM((16, 128), F32),
            pltpu.VMEM((128, 1024), BF),
            pltpu.VMEM((DEPTH, 16, 128), F32),
            pltpu.VMEM((256, 1024), BF),
            pltpu.VMEM((256, 2048), BF),
            pltpu.VMEM((256, 1024), F32),
            pltpu.VMEM((256, 1024), BF),
            pltpu.VMEM((256, 1024), BF),
            pltpu.VMEM((256, 1024), BF),
            pltpu.VMEM((256, 1024), BF),
            pltpu.VMEM((128, 1024), BF),
            pltpu.VMEM((DEPTH, 16, 1024), BF),
            dma(2, 4),
            dma(3),
            dma(2, 4),
            dma(2, 4),
            dma(2, 4),
            dma(2, 4),
            dma(PLANE),
            dma(PLANE),
            dma(2, 4),
            dma(2, 4),
            dma(2, 4),
            dma(2, 4),
            dma(PLANE),
            dma(2, 8),
            dma(2),
            dma(DEPTH),
            dma(DEPTH),
            dma(DEPTH),
            dma(DEPTH),
            dma(PLANE),
            dma(PLANE),
            dma(PLANE),
            dma(PLANE),
            dma(2),
            dma(2),
            dma(PLANE),
            dma(PLANE),
            dma(DEPTH),
            dma(DEPTH),
        ],
        compiler_params=pltpu.CompilerParams(
            collective_id=0, has_side_effects=True, vmem_limit_bytes=VMEM_LIMIT
        ),
    )(*operands)


def local(
    queries,
    new_keys,
    new_values,
    key_cache,
    value_cache,
    lengths,
    residual,
    out_weight,
    norm_gain,
    route_ids,
    route_weights,
    expert_in,
    expert_out,
):
    requests, span = key_cache.shape[:2]
    return layer(
        span,
        queries.reshape(requests, 64, 128),
        new_keys.reshape(requests, 8, 128),
        new_values.reshape(requests, 8, 128),
        key_cache.reshape(requests, 2 * span, 128),
        value_cache.reshape(requests, 2 * span, 128),
        lengths,
        residual,
        out_weight,
        norm_gain.reshape(1, -1),
        route_ids.T,
        route_weights.T,
        expert_in.reshape(2048, 2, 384),
        expert_out.reshape(384, 2048),
    )


def solution(mesh):
    return jax.shard_map(
        local,
        mesh=mesh,
        in_specs=(
            P("req", "exp", "head", None),
            P("req", "exp", "head", None),
            P("req", "exp", "head", None),
            P("req", "exp", "head", None),
            P("req", "exp", "head", None),
            P("req"),
            P(("req", "exp"), None),
            P("head", "exp"),
            P(),
            P(("req", "exp"), None),
            P(("req", "exp"), None),
            P(("req", "exp"), None, None, "head"),
            P(("req", "exp"), "head", None),
        ),
        out_specs=P(("req", "exp"), "head"),
        check_vma=False,
    )
```

```python
import functools
import math

import jax
import jax.numpy as jnp
from jax import lax
from jax.experimental import pallas as pl
from jax.experimental.pallas import tpu as pltpu
from jax.sharding import PartitionSpec as P

masked_score = -1e30
norm_epsilon = 1e-06
MESH = pl.DeviceIdType.MESH
BF = jnp.bfloat16
F32 = jnp.float32
PLANE = 16
DEPTH = 8
TILE = 256
TURN = 128
VMEM_LIMIT = 60 * 1024 * 1024


def place():
    return lax.axis_index("req"), lax.axis_index("head"), lax.axis_index("exp")


def remote(src, dst, send_sem, recv_sem, target):
    return pltpu.make_async_remote_copy(
        src_ref=src,
        dst_ref=dst,
        send_sem=send_sem,
        recv_sem=recv_sem,
        device_id=target,
        device_id_type=MESH,
    )


def rows16(index):
    return pl.ds(pl.multiple_of(index * 16, 16), 16)


def layer_kernel(
    span,
    q_ref,
    nk_ref,
    nv_ref,
    k_hbm,
    v_hbm,
    len_ref,
    res_ref,
    w_hbm,
    gain_ref,
    ids_ref,
    wts_ref,
    in_hbm,
    down_hbm,
    out_ref,
    raw,
    loose,
    k_ref,
    v_ref,
    bias,
    qbuf,
    scores_a,
    scores_b,
    probs_a,
    probs_b,
    stage,
    recv,
    split,
    flat,
    abuf,
    w_ref,
    pstage,
    pbuf,
    hid_ref,
    sq_stage,
    sq_recv,
    norm_ref,
    in_raw,
    in_ref,
    down_ref,
    meta_ref,
    zbuf,
    mbuf,
    xstage,
    xbuf,
    own_ref,
    ystage,
    ybuf,
    rstage,
    rbuf,
    cstage,
    cbuf,
    kv_sems,
    w_sems,
    q_send,
    q_recv,
    f_send,
    f_recv,
    s_send,
    s_recv,
    a_send,
    a_recv,
    g_send,
    g_recv,
    k_send,
    k_recv,
    p_send,
    p_recv,
    sq_sems,
    z_send,
    z_recv,
    m_send,
    m_recv,
    x_send,
    x_recv,
    h_send,
    h_recv,
    y_send,
    y_recv,
    r_send,
    r_recv,
    c_send,
    c_recv,
):
    after = []
    z, c, me = place()
    other = 1 - c
    row_x = lax.div(me, 4)
    row_y = lax.rem(me, 4)

    sign = 1 - 2 * lax.rem(row_x + row_y, 2)

    def moved(way, step_x, step_y):
        return lax.rem(row_x + way * step_x + 4, 4), lax.rem(row_y + way * step_y + 4, 4)

    def steps(k):
        step_x = lax.rem(k, 4)
        return step_x, lax.rem(step_x + lax.div(k, 4), 4)

    def partner(k):
        to_x, to_y = moved(sign, *steps(k))
        return to_x * 4 + to_y

    def origin(k):
        step_x, step_y = steps(k)
        from_x, from_y = moved(sign * (2 * lax.rem(step_x + step_y, 2) - 1), step_x, step_y)
        return from_x * 4 + from_y

    def kv_copy(which, request):
        source = (k_hbm, v_hbm)[which]
        return pltpu.make_async_copy(
            source.at[request], raw.at[which, request], kv_sems.at[which, request]
        )

    def w_copy(which):
        held = (w_ref.at[row_y], in_raw, down_ref)[which]
        source, target = (w_hbm, in_hbm, down_hbm)[which], held
        return pltpu.make_async_copy(source, target, w_sems.at[which])

    barrier = pltpu.get_barrier_semaphore()

    def greet(*target):
        pl.semaphore_signal(barrier, inc=1, device_id=target, device_id_type=MESH)

    @pl.loop(1, PLANE)
    def _(i):
        peer = lax.rem(me + i, PLANE)
        greet(z, c, peer)

    @pl.loop(1, DEPTH)
    def _(i):
        greet(lax.rem(z + i, DEPTH), c, me)

    @pl.loop(0, 4)
    def _(i):
        greet(z, other, i * 4 + row_y)

    @pl.loop(0, 4)
    def _(i):
        request = lax.rem(2 + i, 4)
        kv_copy(0, request).start()
        kv_copy(1, request).start()

    for which in range(3):
        w_copy(which).start()

    meta_ref[...] = jnp.zeros((16, 128), F32)
    meta_ref[0:8, 0:16] = ids_ref[...].astype(F32)
    meta_ref[8:16, 0:16] = wts_ref[...]
    meta_ref[...] = pltpu.roll(meta_ref[...], 16 * z, 1)
    pl.semaphore_wait(barrier, PLANE - 1 + 4 + DEPTH - 1)

    def q_copy(axis, source, target):
        span_rows = pl.ds(2 * axis, 2)
        if axis == 0:
            block, device = (source, row_y), (z, c, target * 4 + row_y)
        else:
            block, device = (row_x, source), (z, c, row_x * 4 + target)
        cols = pl.ds(pl.multiple_of(block[1] * 64, 64), 64)
        return remote(
            q_ref.at[span_rows],
            qbuf.at[span_rows, block[0], cols, :],
            q_send.at[axis, target],
            q_recv.at[axis, source],
            device,
        )

    @pl.loop(1, 4)
    def _(i):
        q_copy(1, row_y, lax.rem(row_y + i, 4)).start()
        q_copy(0, row_x, lax.rem(row_x + i, 4)).start()

    @after.append
    def _():
        @pl.loop(1, 4)
        def _(i):
            q_copy(0, row_x, lax.rem(row_x + i, 4)).wait_send()
            q_copy(1, row_y, lax.rem(row_y + i, 4)).wait_send()

    def m_copy(source, target):
        return remote(
            meta_ref, mbuf.at[source], m_send.at[target], m_recv.at[source], (target, c, me)
        )

    @pl.loop(1, DEPTH)
    def _(i):
        m_copy(z, lax.rem(z + i, DEPTH)).start()

    @after.append
    def _():
        @pl.loop(1, DEPTH)
        def _(i):
            m_copy(z, lax.rem(z + i, DEPTH)).wait_send()

    mbuf[z] = meta_ref[...]
    qbuf[:, row_x, pl.ds(pl.multiple_of(row_y * 64, 64), 64), :] = q_ref[...]

    def f_copy(axis, source, target):
        if axis == 0:
            cols = pl.ds(pl.multiple_of(source * 64, 64), 64)
            block, device = qbuf.at[0:2, :, cols, :], (z, c, row_x * 4 + target)
        else:
            block, device = qbuf.at[2:4, source, :, :], (z, c, target * 4 + row_y)
        return remote(block, block, f_send.at[axis, target], f_recv.at[axis, source], device)

    keys = span + 128
    key_iota = lax.broadcasted_iota(jnp.int32, (8, keys), 1)

    def arrange(request):
        cached = jnp.logical_and(key_iota < span, key_iota + me * span < len_ref[request])
        fresh = jnp.logical_and(key_iota >= span, key_iota < span + 4)
        bias[request] = jnp.where(jnp.logical_or(cached, fresh), 0.0, masked_score)
        for which in range(2):
            target = (k_ref, v_ref)[which]
            new = (nk_ref, nv_ref)[which]
            kv_copy(which, request).wait()

            @pl.loop(0, span // TILE)
            def _(i):
                rows = pl.ds(pl.multiple_of(i * 2 * TILE, 2 * TILE), 2 * TILE)
                loose[...] = raw[which, request, rows, :].astype(F32)
                into = pl.ds(pl.multiple_of(i * TILE, TILE), TILE)
                target[request, into, 0:128] = loose[pl.ds(0, TILE, 2), :].astype(BF)
                target[request, into, 128:256] = loose[pl.ds(1, TILE, 2), :].astype(BF)

            loose[0:8, :] = new[request].astype(F32)
            loose[8:256, :] = jnp.zeros((248, 128), F32)
            tail = pl.ds(span, 128)
            target[request, tail, 0:128] = loose[pl.ds(0, 128, 2), :].astype(BF)
            target[request, tail, 128:256] = loose[pl.ds(1, 128, 2), :].astype(BF)

    arrange(2)

    @pl.loop(1, 4)
    def _(i):
        q_copy(1, lax.rem(row_y + i, 4), row_y).wait_recv()

    @pl.loop(1, 4)
    def _(i):
        f_copy(1, row_x, lax.rem(row_x + i, 4)).start()

    @pl.loop(1, 4)
    def _(i):
        q_copy(0, lax.rem(row_x + i, 4), row_x).wait_recv()

    @pl.loop(1, 4)
    def _(i):
        f_copy(0, row_y, lax.rem(row_y + i, 4)).start()

    @after.append
    def _():
        @pl.loop(1, 4)
        def _(i):
            f_copy(0, row_y, lax.rem(row_y + i, 4)).wait_send()
            f_copy(1, row_x, lax.rem(row_x + i, 4)).wait_send()

    def w_rows(side, batch):
        return pl.ds(pl.multiple_of(lax.rem(side, 2) * 1024 + batch * 512, 512), 512)

    def g_copy(source, target, batch):
        return remote(
            w_ref.at[source, w_rows(z, batch)],
            w_ref.at[source, w_rows(z, batch)],
            g_send.at[batch, target],
            g_recv.at[batch, source],
            (z, c, row_x * 4 + target),
        )

    def k_copy(side, part, batch):
        rows = w_rows(side, batch)
        return remote(
            w_ref.at[part, rows],
            w_ref.at[part, rows],
            k_send.at[batch, part],
            k_recv.at[batch, part],
            (z + 1 - 2 * lax.rem(z, 2), c, me),
        )

    w_copy(0).wait()

    for batch in range(2):

        @pl.loop(1, 4)
        def _(i):
            g_copy(row_y, lax.rem(row_y + i, 4), batch).start()

    @after.append
    def _():
        @pl.loop(1, 4)
        def _(i):
            for batch in range(2):
                g_copy(row_y, lax.rem(row_y + i, 4), batch).wait_send()
                k_copy(z, lax.rem(row_y + i, 4), batch).wait_send()

    arrange(3)
    arrange(0)
    arrange(1)

    @pl.loop(1, 4)
    def _(i):
        f_copy(1, lax.rem(row_x + i, 4), row_x).wait_recv()
        f_copy(0, lax.rem(row_y + i, 4), row_y).wait_recv()

    row_iota = lax.broadcasted_iota(jnp.int32, (256, 128), 0)
    low = lax.rem(row_iota, 16) < 8
    low_mask = jnp.where(low, 1.0, 0.0).astype(BF)
    high_mask = jnp.where(low, 0.0, 1.0).astype(BF)
    stat_iota = lax.broadcasted_iota(jnp.int32, (16, 128), 0)
    factor = (128.0 ** -0.5) * math.log2(math.e)
    tiles = [slice(t * 128, t * 128 + 128) for t in range(keys // 128)]

    def s_copy(owner, source):
        return remote(
            stage.at[owner],
            recv.at[source],
            s_send.at[owner],
            s_recv.at[source],
            (z, c, owner),
        )

    def score(request, group, scores):
        q = qbuf[request, group]
        both = jnp.concatenate([q * low_mask, q * high_mask], axis=1)
        scores[...] = lax.dot_general(
            both, k_ref[request], (((1,), (1,)), ((), ())), preferred_element_type=F32
        )

    def soften(request, scores, probs):
        levels, totals = [], []
        for part in range(2):
            rows = slice(part * 128, part * 128 + 128)
            top = scores[rows, tiles[0]] + bias[request, 0:1, tiles[0]]
            for tile in tiles[1:]:
                top = jnp.maximum(top, scores[rows, tile] + bias[request, 0:1, tile])
            shift = jnp.max(top, axis=1, keepdims=True) * factor
            total = jnp.zeros((128, 128), F32)
            for tile in tiles:
                shown = scores[rows, tile] + bias[request, 0:1, tile]
                prob = jnp.exp2(shown * factor - shift)
                total = total + prob
                probs[rows, tile] = prob.astype(BF)
            total = jnp.sum(total, axis=1, keepdims=True)
            levels.append(shift + jnp.log2(total))
            totals.append(total)
        return jnp.concatenate(levels, axis=0), jnp.concatenate(totals, axis=0)

    def finish(owner, request, probs, level, total):
        sums = jnp.dot(probs[...], v_ref[request], preferred_element_type=F32)
        mean = jnp.where(low, sums[:, :128], sums[:, 128:]) / total
        turned = jnp.transpose(jnp.broadcast_to(level, (256, 128)))[0:1, :]
        stats = jnp.zeros((16, 128), F32)
        for half in range(2):
            rest = turned[:, half * 128 : half * 128 + 128]
            for term in range(3):
                part = rest.astype(BF).astype(F32)
                rest = rest - part
                stats = jnp.where(stat_iota == 2 * term + half, part, stats)
        stage[owner, 0:256, :] = mean.astype(BF)
        stage[owner, 256:272, :] = stats.astype(BF)

        @pl.when(owner != me)
        def _():
            s_copy(owner, me).start()

    @after.append
    def _():
        @pl.loop(1, PLANE)
        def _(i):
            s_copy(lax.rem(me + i, PLANE), me).wait_send()

    @pl.loop(0, PLANE // 2)
    def _(i):
        for batch in range(2):

            @pl.when(i == 3 + 2 * batch)
            def _():
                @pl.loop(1, 4)
                def _(k):
                    g_copy(lax.rem(row_y + k, 4), row_y, batch).wait_recv()
                    k_copy(z, lax.rem(row_y + k, 4), batch).start()

        step_x = lax.rem(lax.div(i, 2) + 1, 4)
        request, group_a = moved(sign, step_x, 2 + lax.rem(i, 2))
        group_b = moved(sign, step_x, 1 - lax.rem(i, 2))[1]
        score(request, group_a, scores_a)
        score(request, group_b, scores_b)
        level_a, total_a = soften(request, scores_a, probs_a)
        finish(request * 4 + group_a, request, probs_a, level_a, total_a)
        level_b, total_b = soften(request, scores_b, probs_b)
        finish(request * 4 + group_b, request, probs_b, level_b, total_b)

    recv[me] = stage[me]

    @pl.loop(1, PLANE)
    def _(i):
        s_copy(me, lax.rem(me + i, PLANE)).wait_recv()

    terms = recv[:, 256:272, :].astype(F32)
    term_iota = lax.broadcasted_iota(jnp.int32, (16, 16, 128), 1)
    columns = []
    for half in range(2):
        mine = jnp.logical_and(term_iota < 6, lax.rem(term_iota, 2) == half)
        level = jnp.sum(jnp.where(mine, terms, 0.0), axis=1)
        weight = jnp.exp2(level - jnp.max(level, axis=0, keepdims=True))
        weight = weight / jnp.sum(weight, axis=0, keepdims=True)
        padded = jnp.concatenate([weight, jnp.zeros((112, 128), F32)], axis=0)
        columns.append(jnp.transpose(padded))
    weights = jnp.concatenate(columns, axis=0)
    merged = jnp.zeros((256, 128), F32)
    for source in range(PLANE):
        merged = merged + weights[:, source : source + 1] * recv[source, 0:256, :].astype(F32)
    split[...] = merged.reshape(16, 16, 128)
    for head in range(16):
        flat[:, head * 128 : head * 128 + 128] = split[:, head, :].astype(BF)

    def a_copy(source, target):
        return remote(
            flat,
            abuf.at[rows16(source), :],
            a_send.at[target],
            a_recv.at[source],
            (z, c, target * 4 + row_y),
        )

    @pl.loop(1, 4)
    def _(i):
        a_copy(row_x, lax.rem(row_x + i, 4)).start()

    abuf[rows16(row_x), :] = flat[...]

    @after.append
    def _():
        @pl.loop(1, 4)
        def _(i):
            a_copy(row_x, lax.rem(row_x + i, 4)).wait_send()

    @pl.loop(1, DEPTH)
    def _(i):
        m_copy(lax.rem(z + i, DEPTH), z).wait_recv()

    meta = jnp.sum(mbuf[...], axis=0)
    expert_iota = lax.broadcasted_iota(jnp.int32, (16, 128), 0).astype(F32)
    expert_iota = expert_iota + (z * PLANE).astype(F32)
    named = jnp.zeros((16, 128), F32)
    weight = jnp.zeros((16, 128), F32)
    for k in range(8):
        hit = meta[k : k + 1, :] == expert_iota
        named = named + jnp.where(hit, 1.0, 0.0)
        weight = weight + jnp.where(hit, meta[8 + k : 9 + k, :], 0.0)
    from_row = lax.broadcasted_iota(jnp.int32, (128, 128), 0)
    to_row = lax.broadcasted_iota(jnp.int32, (128, 128), 1)
    same = lax.div(from_row, 16) == lax.div(to_row, 16)
    earlier = jnp.where(jnp.logical_and(same, from_row < to_row), 1.0, 0.0).astype(BF)
    rank = jnp.dot(named.astype(BF), earlier, preferred_element_type=F32)
    slot = 2.0 * lax.div(lax.broadcasted_iota(jnp.int32, (16, 128), 1), 16).astype(F32) + rank
    slot = jnp.where(named > 0.5, slot, -1.0)
    slot_iota = lax.broadcasted_iota(jnp.int32, (16, 16, 128), 1).astype(F32)
    chosen = slot[:, None, :] == slot_iota
    placing = jnp.where(chosen, 1.0, 0.0).reshape(256, 128).astype(BF)
    scaled = jnp.where(chosen, weight[:, None, :], 0.0).reshape(256, 128)
    turned = jnp.transpose(scaled)
    turned_high = turned.astype(BF)
    turned_low = (turned - turned_high.astype(F32)).astype(BF)

    @pl.loop(1, 4)
    def _(i):
        k_copy(z + 1, lax.rem(row_y + i, 4), 0).wait_recv()
        k_copy(z + 1, lax.rem(row_y + i, 4), 1).wait_recv()

    @pl.loop(1, 4)
    def _(i):
        a_copy(lax.rem(row_x + i, 4), row_x).wait_recv()

    gathered = abuf[...]
    for part in range(4):
        columns = jnp.dot(gathered, w_ref[part], preferred_element_type=F32)
        pstage[:, :, part * 128 : part * 128 + 128] = columns.reshape(4, 16, 128)
    own_side = lax.div(row_x, 2)

    def p_copy(source_core, source, target):
        return remote(
            pstage.at[target],
            pbuf.at[source_core, lax.rem(source, 2)],
            p_send.at[target],
            p_recv.at[source_core, lax.rem(source, 2)],
            (z, lax.div(source, 2), target * 4 + row_y),
        )

    @pl.loop(1, 4)
    def _(i):
        p_copy(c, row_x, lax.rem(row_x + i, 4)).start()

    @pl.when(own_side != c)
    def _():
        p_copy(c, row_x, row_x).start()

    @pl.when(own_side == c)
    def _():
        pbuf[c, lax.rem(row_x, 2)] = pstage[row_x]

    @after.append
    def _():
        @pl.loop(1, 4)
        def _(i):
            p_copy(c, row_x, lax.rem(row_x + i, 4)).wait_send()

        @pl.when(own_side != c)
        def _():
            p_copy(c, row_x, row_x).wait_send()

    @pl.loop(0, 2)
    def _(i):
        p_copy(other, c * 2 + i, row_x).wait_recv()

        @pl.when(c * 2 + i != row_x)
        def _():
            p_copy(c, c * 2 + i, row_x).wait_recv()

    mine = pl.ds(pl.multiple_of(c * 1024, 1024), 1024)
    theirs = pl.ds(pl.multiple_of(other * 1024, 1024), 1024)
    square = jnp.zeros((16, 128), F32)
    for part in range(8):
        cols = pl.ds(pl.multiple_of(c * 1024 + part * 128, 128), 128)
        inner = slice(part % 4 * 128, part % 4 * 128 + 128)
        arrived = pbuf[0, part // 4, :, inner] + pbuf[1, part // 4, :, inner]
        hidden = res_ref[:, cols].astype(F32) + arrived
        hid_ref[:, part * 128 : part * 128 + 128] = hidden
        square = square + hidden * hidden
    sq_stage[...] = square
    sq_copy = remote(sq_stage, sq_recv, sq_sems.at[0], sq_sems.at[1], (z, other, me))
    sq_copy.start()
    after.append(sq_copy.wait_send)
    scaled_hidden = hid_ref[...] * gain_ref[:, mine]
    sq_copy.wait_recv()
    square = square + sq_recv[...]
    mean_square = jnp.sum(square, axis=1, keepdims=True) * (1.0 / 2048.0)
    norm_ref[...] = (scaled_hidden * lax.rsqrt(mean_square + norm_epsilon)).astype(BF)

    def z_copy(source, target):
        return remote(
            norm_ref, zbuf.at[rows16(source), :], z_send.at[target], z_recv.at[source], (target, c, me)
        )

    @pl.loop(1, DEPTH)
    def _(i):
        z_copy(z, lax.rem(z + i, DEPTH)).start()

    @after.append
    def _():
        @pl.loop(1, DEPTH)
        def _(i):
            z_copy(z, lax.rem(z + i, DEPTH)).wait_send()

    zbuf[rows16(z), :] = norm_ref[...]
    w_copy(1).wait()

    @pl.loop(0, 2048 // TURN)
    def _(i):
        rows = pl.ds(pl.multiple_of(i * TURN, TURN), TURN)
        for side in range(2):
            in_ref[rows, side * 384 : side * 384 + 384] = in_raw[rows, side, :]

    w_copy(2).wait()

    @pl.loop(1, DEPTH)
    def _(i):
        z_copy(lax.rem(z + i, DEPTH), z).wait_recv()

    xstage[...] = jnp.dot(placing, zbuf[...], preferred_element_type=F32).astype(BF)

    def x_copy(step):
        target = partner(step)
        return remote(
            xstage.at[rows16(target), :],
            xbuf.at[rows16(step), mine],
            x_send.at[step],
            x_recv.at[step],
            (z, c, target),
        )

    def h_copy(step, columns):
        block = xbuf.at[rows16(step), columns]
        return remote(block, block, h_send.at[step], h_recv.at[step], (z, other, me))

    def y_copy(half):
        rows = pl.ds(half * 128, 128)
        return remote(
            ystage.at[rows, :], ybuf.at[rows, :], y_send.at[half], y_recv.at[half], (z, other, me)
        )

    def r_copy(step, expert):
        return remote(
            rstage.at[rows16(step), :],
            rbuf.at[rows16(expert), :],
            r_send.at[step],
            r_recv.at[step],
            (z, c, origin(step)),
        )

    def forward(start, stop):
        @pl.loop(start, stop)
        def _(i):
            x_copy(i).wait_recv()
            h_copy(i, mine).start()

    def evaluate(half):
        @pl.loop(8 * half, 8 * half + 8)
        def _(i):
            h_copy(i, theirs).wait_recv()

        rows = slice(128 * half, 128 * half + 128)
        gate_up = jnp.dot(xbuf[rows, :], in_ref[...], preferred_element_type=F32)
        gate = gate_up[:, :384]
        active = (gate / (1.0 + jnp.exp(-gate)) * gate_up[:, 384:]).astype(BF)
        partial = jnp.dot(active, down_ref[:, theirs], preferred_element_type=F32)
        ystage[rows, :] = partial.astype(BF)
        y_copy(half).start()
        own_ref[rows, :] = jnp.dot(active, down_ref[:, mine], preferred_element_type=F32)

    def give_back(half):
        rows = slice(128 * half, 128 * half + 128)
        y_copy(half).wait_recv()
        rstage[rows, :] = (own_ref[rows, :] + ybuf[rows, :].astype(F32)).astype(BF)

        @pl.loop(max(1, 8 * half), 8 * half + 8)
        def _(i):
            r_copy(i, me).start()

    @pl.loop(1, PLANE)
    def _(i):
        x_copy(i).start()

    @after.append
    def _():
        @pl.loop(1, PLANE)
        def _(i):
            x_copy(i).wait_send()

    @after.append
    def _():
        @pl.loop(0, PLANE)
        def _(i):
            h_copy(i, mine).wait_send()

    xbuf[0:16, mine] = xstage[rows16(me), :]
    h_copy(0, mine).start()
    forward(1, 8)
    evaluate(0)
    forward(8, PLANE)
    give_back(0)
    after.append(y_copy(0).wait_send)
    after.append(y_copy(1).wait_send)
    @after.append
    def _():
        @pl.loop(1, PLANE)
        def _(i):
            r_copy(i, me).wait_send()

    rbuf[rows16(me), :] = rstage[0:16, :]
    evaluate(1)
    give_back(1)

    @pl.loop(1, PLANE)
    def _(i):
        r_copy(i, partner(i)).wait_recv()

    mixed = jnp.dot(turned_high, rbuf[...], preferred_element_type=F32)
    mixed = mixed + jnp.dot(turned_low, rbuf[...], preferred_element_type=F32)
    cstage[...] = mixed.astype(BF)

    def c_copy(source, target):
        return remote(
            cstage.at[rows16(target), :],
            cbuf.at[source],
            c_send.at[target],
            c_recv.at[source],
            (target, c, me),
        )

    @pl.loop(1, DEPTH)
    def _(i):
        c_copy(z, lax.rem(z + i, DEPTH)).start()

    @after.append
    def _():
        @pl.loop(1, DEPTH)
        def _(i):
            c_copy(z, lax.rem(z + i, DEPTH)).wait_send()

    cbuf[z] = cstage[rows16(z), :]

    @pl.loop(1, DEPTH)
    def _(i):
        c_copy(lax.rem(z + i, DEPTH), z).wait_recv()

    total = hid_ref[...]
    for source in range(DEPTH):
        total = total + cbuf[source].astype(F32)
    out_ref[...] = total.astype(BF)

    for settle in after:
        settle()


def dma(*shape):
    return pltpu.SemaphoreType.DMA(shape)


def layer(span, *operands):
    specs = [pl.BlockSpec(memory_space=pltpu.VMEM)] * 13
    for held in (3, 4, 7, 11, 12):
        specs[held] = pl.BlockSpec(memory_space=pl.ANY)
    specs[5] = pl.BlockSpec(memory_space=pltpu.SMEM)
    keys = span + 128
    return pl.pallas_call(
        functools.partial(layer_kernel, span),
        out_shape=jax.ShapeDtypeStruct((16, 1024), BF),
        in_specs=specs,
        out_specs=pl.BlockSpec(memory_space=pltpu.VMEM),
        scratch_shapes=[
            pltpu.VMEM((2, 4, 2 * span, 128), BF),
            pltpu.VMEM((2 * TILE, 128), F32),
            pltpu.VMEM((4, keys, 256), BF),
            pltpu.VMEM((4, keys, 256), BF),
            pltpu.VMEM((4, 8, keys), F32),
            pltpu.VMEM((4, 4, 256, 128), BF),
            pltpu.VMEM((256, keys), F32),
            pltpu.VMEM((256, keys), F32),
            pltpu.VMEM((256, keys), BF),
            pltpu.VMEM((256, keys), BF),
            pltpu.VMEM((PLANE, 272, 128), BF),
            pltpu.VMEM((PLANE, 272, 128), BF),
            pltpu.VMEM((16, 16, 128), F32),
            pltpu.VMEM((16, 2048), BF),
            pltpu.VMEM((64, 2048), BF),
            pltpu.VMEM((4, 2048, 128), BF),
            pltpu.VMEM((4, 16, 512), F32),
            pltpu.VMEM((2, 2, 16, 512), F32),
            pltpu.VMEM((16, 1024), F32),
            pltpu.VMEM((16, 128), F32),
            pltpu.VMEM((16, 128), F32),
            pltpu.VMEM((16, 1024), BF),
            pltpu.VMEM((2048, 2, 384), BF),
            pltpu.VMEM((2048, 768), BF),
            pltpu.VMEM((384, 2048), BF),
            pltpu.VMEM((16, 128), F32),
            pltpu.VMEM((128, 1024), BF),
            pltpu.VMEM((DEPTH, 16, 128), F32),
            pltpu.VMEM((256, 1024), BF),
            pltpu.VMEM((256, 2048), BF),
            pltpu.VMEM((256, 1024), F32),
            pltpu.VMEM((256, 1024), BF),
            pltpu.VMEM((256, 1024), BF),
            pltpu.VMEM((256, 1024), BF),
            pltpu.VMEM((256, 1024), BF),
            pltpu.VMEM((128, 1024), BF),
            pltpu.VMEM((DEPTH, 16, 1024), BF),
            dma(2, 4),
            dma(3),
            dma(2, 4),
            dma(2, 4),
            dma(2, 4),
            dma(2, 4),
            dma(PLANE),
            dma(PLANE),
            dma(4),
            dma(4),
            dma(2, 4),
            dma(2, 4),
            dma(2, 4),
            dma(2, 4),
            dma(4),
            dma(2, 2),
            dma(2),
            dma(DEPTH),
            dma(DEPTH),
            dma(DEPTH),
            dma(DEPTH),
            dma(PLANE),
            dma(PLANE),
            dma(PLANE),
            dma(PLANE),
            dma(2),
            dma(2),
            dma(PLANE),
            dma(PLANE),
            dma(DEPTH),
            dma(DEPTH),
        ],
        compiler_params=pltpu.CompilerParams(
            collective_id=0, has_side_effects=True, vmem_limit_bytes=VMEM_LIMIT
        ),
    )(*operands)


def local(
    queries,
    new_keys,
    new_values,
    key_cache,
    value_cache,
    lengths,
    residual,
    out_weight,
    norm_gain,
    route_ids,
    route_weights,
    expert_in,
    expert_out,
):
    requests, span = key_cache.shape[:2]
    return layer(
        span,
        queries.reshape(requests, 64, 128),
        new_keys.reshape(requests, 8, 128),
        new_values.reshape(requests, 8, 128),
        key_cache.reshape(requests, 2 * span, 128),
        value_cache.reshape(requests, 2 * span, 128),
        lengths,
        residual,
        out_weight,
        norm_gain.reshape(1, -1),
        route_ids.T,
        route_weights.T,
        expert_in.reshape(2048, 2, 384),
        expert_out.reshape(384, 2048),
    )


def solution(mesh):
    return jax.shard_map(
        local,
        mesh=mesh,
        in_specs=(
            P("req", "exp", "head", None),
            P("req", "exp", "head", None),
            P("req", "exp", "head", None),
            P("req", "exp", "head", None),
            P("req", "exp", "head", None),
            P("req"),
            P(("req", "exp"), None),
            P("head", "exp"),
            P(),
            P(("req", "exp"), None),
            P(("req", "exp"), None),
            P(("req", "exp"), None, None, "head"),
            P(("req", "exp"), "head", None),
        ),
        out_specs=P(("req", "exp"), "head"),
        check_vma=False,
    )
```

```python
import functools
import math

import jax
import jax.numpy as jnp
from jax import lax
from jax.experimental import pallas as pl
from jax.experimental.pallas import tpu as pltpu
from jax.sharding import PartitionSpec as P

masked_score = -1e30
norm_epsilon = 1e-06
MESH = pl.DeviceIdType.MESH
BF = jnp.bfloat16
F32 = jnp.float32
PLANE = 16
DEPTH = 8
TILE = 256
TURN = 128
VMEM_LIMIT = 60 * 1024 * 1024


def place():
    return lax.axis_index("req"), lax.axis_index("head"), lax.axis_index("exp")


def remote(src, dst, send_sem, recv_sem, target):
    return pltpu.make_async_remote_copy(
        src_ref=src,
        dst_ref=dst,
        send_sem=send_sem,
        recv_sem=recv_sem,
        device_id=target,
        device_id_type=MESH,
    )


def rows16(index):
    return pl.ds(pl.multiple_of(index * 16, 16), 16)


def layer_kernel(
    span,
    q_ref,
    nk_ref,
    nv_ref,
    k_hbm,
    v_hbm,
    len_ref,
    res_ref,
    w_hbm,
    gain_ref,
    ids_ref,
    wts_ref,
    in_hbm,
    down_hbm,
    out_ref,
    raw,
    loose,
    k_ref,
    v_ref,
    bias,
    qbuf,
    scores_a,
    scores_b,
    probs_a,
    probs_b,
    stage,
    recv,
    split,
    flat,
    abuf,
    w_ref,
    pstage,
    pbuf,
    hid_ref,
    sq_stage,
    sq_recv,
    norm_ref,
    in_raw,
    in_ref,
    down_ref,
    meta_ref,
    zbuf,
    mbuf,
    xstage,
    xbuf,
    own_ref,
    ystage,
    ybuf,
    rstage,
    rbuf,
    cstage,
    cbuf,
    kv_sems,
    w_sems,
    q_send,
    q_recv,
    f_send,
    f_recv,
    s_send,
    s_recv,
    a_send,
    a_recv,
    g_send,
    g_recv,
    k_send,
    k_recv,
    p_send,
    p_recv,
    sq_sems,
    z_send,
    z_recv,
    m_send,
    m_recv,
    x_send,
    x_recv,
    h_send,
    h_recv,
    y_send,
    y_recv,
    r_send,
    r_recv,
    c_send,
    c_recv,
):
    after = []
    z, c, me = place()
    other = 1 - c
    row_x = lax.div(me, 4)
    row_y = lax.rem(me, 4)

    def far_first(i):
        near = DEPTH - i
        half = lax.div(near + 1, 2)
        odd = lax.rem(near, 2)
        return odd * half + (1 - odd) * (DEPTH - half)

    sign = 1 - 2 * lax.rem(row_x + row_y, 2)

    def moved(way, step_x, step_y):
        return lax.rem(row_x + way * step_x + 4, 4), lax.rem(row_y + way * step_y + 4, 4)

    def steps(k):
        step_x = lax.rem(k, 4)
        return step_x, lax.rem(step_x + lax.div(k, 4), 4)

    def partner(k):
        to_x, to_y = moved(sign, *steps(k))
        return to_x * 4 + to_y

    def origin(k):
        step_x, step_y = steps(k)
        from_x, from_y = moved(sign * (2 * lax.rem(step_x + step_y, 2) - 1), step_x, step_y)
        return from_x * 4 + from_y

    def kv_copy(which, request):
        source = (k_hbm, v_hbm)[which]
        return pltpu.make_async_copy(
            source.at[request], raw.at[which, request], kv_sems.at[which, request]
        )

    def w_copy(which):
        held = (w_ref.at[row_y], in_raw, down_ref)[which]
        source, target = (w_hbm, in_hbm, down_hbm)[which], held
        return pltpu.make_async_copy(source, target, w_sems.at[which])

    barrier = pltpu.get_barrier_semaphore()

    def greet(*target):
        pl.semaphore_signal(barrier, inc=1, device_id=target, device_id_type=MESH)

    @pl.loop(1, PLANE)
    def _(i):
        peer = lax.rem(me + i, PLANE)
        greet(z, c, peer)

    @pl.loop(1, DEPTH)
    def _(i):
        greet(lax.rem(z + i, DEPTH), c, me)

    @pl.loop(0, 4)
    def _(i):
        greet(z, other, i * 4 + row_y)

    @pl.loop(0, 4)
    def _(i):
        request = lax.rem(2 + i, 4)
        kv_copy(0, request).start()
        kv_copy(1, request).start()

    for which in range(3):
        w_copy(which).start()

    meta_ref[...] = jnp.zeros((16, 128), F32)
    meta_ref[0:8, 0:16] = ids_ref[...].astype(F32)
    meta_ref[8:16, 0:16] = wts_ref[...]
    meta_ref[...] = pltpu.roll(meta_ref[...], 16 * z, 1)
    pl.semaphore_wait(barrier, PLANE - 1 + 4 + DEPTH - 1)

    def q_copy(axis, source, target):
        span_rows = pl.ds(2 * axis, 2)
        if axis == 0:
            block, device = (source, row_y), (z, c, target * 4 + row_y)
        else:
            block, device = (row_x, source), (z, c, row_x * 4 + target)
        cols = pl.ds(pl.multiple_of(block[1] * 64, 64), 64)
        return remote(
            q_ref.at[span_rows],
            qbuf.at[span_rows, block[0], cols, :],
            q_send.at[axis, target],
            q_recv.at[axis, source],
            device,
        )

    @pl.loop(1, 4)
    def _(i):
        q_copy(1, row_y, lax.rem(row_y + i, 4)).start()
        q_copy(0, row_x, lax.rem(row_x + i, 4)).start()

    @after.append
    def _():
        @pl.loop(1, 4)
        def _(i):
            q_copy(0, row_x, lax.rem(row_x + i, 4)).wait_send()
            q_copy(1, row_y, lax.rem(row_y + i, 4)).wait_send()

    def m_copy(source, target):
        return remote(
            meta_ref, mbuf.at[source], m_send.at[target], m_recv.at[source], (target, c, me)
        )

    @pl.loop(1, DEPTH)
    def _(i):
        m_copy(z, lax.rem(z + i, DEPTH)).start()

    @after.append
    def _():
        @pl.loop(1, DEPTH)
        def _(i):
            m_copy(z, lax.rem(z + i, DEPTH)).wait_send()

    mbuf[z] = meta_ref[...]
    qbuf[:, row_x, pl.ds(pl.multiple_of(row_y * 64, 64), 64), :] = q_ref[...]

    def f_copy(axis, source, target):
        if axis == 0:
            cols = pl.ds(pl.multiple_of(source * 64, 64), 64)
            block, device = qbuf.at[0:2, :, cols, :], (z, c, row_x * 4 + target)
        else:
            block, device = qbuf.at[2:4, source, :, :], (z, c, target * 4 + row_y)
        return remote(block, block, f_send.at[axis, target], f_recv.at[axis, source], device)

    keys = span + 128
    key_iota = lax.broadcasted_iota(jnp.int32, (8, keys), 1)

    def arrange(request):
        cached = jnp.logical_and(key_iota < span, key_iota + me * span < len_ref[request])
        fresh = jnp.logical_and(key_iota >= span, key_iota < span + 4)
        bias[request] = jnp.where(jnp.logical_or(cached, fresh), 0.0, masked_score)
        for which in range(2):
            target = (k_ref, v_ref)[which]
            new = (nk_ref, nv_ref)[which]
            kv_copy(which, request).wait()

            @pl.loop(0, span // TILE)
            def _(i):
                rows = pl.ds(pl.multiple_of(i * 2 * TILE, 2 * TILE), 2 * TILE)
                loose[...] = raw[which, request, rows, :].astype(F32)
                into = pl.ds(pl.multiple_of(i * TILE, TILE), TILE)
                target[request, into, 0:128] = loose[pl.ds(0, TILE, 2), :].astype(BF)
                target[request, into, 128:256] = loose[pl.ds(1, TILE, 2), :].astype(BF)

            loose[0:8, :] = new[request].astype(F32)
            loose[8:256, :] = jnp.zeros((248, 128), F32)
            tail = pl.ds(span, 128)
            target[request, tail, 0:128] = loose[pl.ds(0, 128, 2), :].astype(BF)
            target[request, tail, 128:256] = loose[pl.ds(1, 128, 2), :].astype(BF)

    def w_rows(side, batch):
        return pl.ds(pl.multiple_of(lax.rem(side, 2) * 1024 + batch * 512, 512), 512)

    def g_copy(source, target, batch):
        return remote(
            w_ref.at[source, w_rows(z, batch)],
            w_ref.at[source, w_rows(z, batch)],
            g_send.at[batch, target],
            g_recv.at[batch, source],
            (z, c, row_x * 4 + target),
        )

    def k_copy(side, part, batch):
        rows = w_rows(side, batch)
        return remote(
            w_ref.at[part, rows],
            w_ref.at[part, rows],
            k_send.at[batch, part],
            k_recv.at[batch, part],
            (z + 1 - 2 * lax.rem(z, 2), c, me),
        )

    w_copy(0).wait()

    for batch in range(2):

        @pl.loop(1, 4)
        def _(i):
            g_copy(row_y, lax.rem(row_y + i, 4), batch).start()

    arrange(2)

    @pl.loop(1, 4)
    def _(i):
        q_copy(1, lax.rem(row_y + i, 4), row_y).wait_recv()

    @pl.loop(1, 4)
    def _(i):
        f_copy(1, row_x, lax.rem(row_x + i, 4)).start()

    @pl.loop(1, 4)
    def _(i):
        q_copy(0, lax.rem(row_x + i, 4), row_x).wait_recv()

    @pl.loop(1, 4)
    def _(i):
        f_copy(0, row_y, lax.rem(row_y + i, 4)).start()

    @after.append
    def _():
        @pl.loop(1, 4)
        def _(i):
            f_copy(0, row_y, lax.rem(row_y + i, 4)).wait_send()
            f_copy(1, row_x, lax.rem(row_x + i, 4)).wait_send()

    @after.append
    def _():
        @pl.loop(1, 4)
        def _(i):
            for batch in range(2):
                g_copy(row_y, lax.rem(row_y + i, 4), batch).wait_send()
                k_copy(z, lax.rem(row_y + i, 4), batch).wait_send()

    arrange(3)
    arrange(0)
    arrange(1)

    @pl.loop(1, 4)
    def _(i):
        f_copy(1, lax.rem(row_x + i, 4), row_x).wait_recv()
        f_copy(0, lax.rem(row_y + i, 4), row_y).wait_recv()

    row_iota = lax.broadcasted_iota(jnp.int32, (256, 128), 0)
    low = lax.rem(row_iota, 16) < 8
    low_mask = jnp.where(low, 1.0, 0.0).astype(BF)
    high_mask = jnp.where(low, 0.0, 1.0).astype(BF)
    stat_iota = lax.broadcasted_iota(jnp.int32, (16, 128), 0)
    factor = (128.0 ** -0.5) * math.log2(math.e)
    tiles = [slice(t * 128, t * 128 + 128) for t in range(keys // 128)]

    def s_copy(owner, source):
        return remote(
            stage.at[owner],
            recv.at[source],
            s_send.at[owner],
            s_recv.at[source],
            (z, c, owner),
        )

    def score(request, group, scores):
        q = qbuf[request, group]
        both = jnp.concatenate([q * low_mask, q * high_mask], axis=1)
        scores[...] = lax.dot_general(
            both, k_ref[request], (((1,), (1,)), ((), ())), preferred_element_type=F32
        )

    def soften(request, scores, probs):
        levels, totals = [], []
        for part in range(2):
            rows = slice(part * 128, part * 128 + 128)
            top = scores[rows, tiles[0]] + bias[request, 0:1, tiles[0]]
            for tile in tiles[1:]:
                top = jnp.maximum(top, scores[rows, tile] + bias[request, 0:1, tile])
            shift = jnp.max(top, axis=1, keepdims=True) * factor
            total = jnp.zeros((128, 128), F32)
            for tile in tiles:
                shown = scores[rows, tile] + bias[request, 0:1, tile]
                prob = jnp.exp2(shown * factor - shift)
                total = total + prob
                probs[rows, tile] = prob.astype(BF)
            total = jnp.sum(total, axis=1, keepdims=True)
            levels.append(shift + jnp.log2(total))
            totals.append(total)
        return jnp.concatenate(levels, axis=0), jnp.concatenate(totals, axis=0)

    def finish(owner, request, probs, level, total):
        sums = jnp.dot(probs[...], v_ref[request], preferred_element_type=F32)
        mean = jnp.where(low, sums[:, :128], sums[:, 128:]) / total
        turned = jnp.transpose(jnp.broadcast_to(level, (256, 128)))[0:1, :]
        stats = jnp.zeros((16, 128), F32)
        for half in range(2):
            rest = turned[:, half * 128 : half * 128 + 128]
            for term in range(3):
                part = rest.astype(BF).astype(F32)
                rest = rest - part
                stats = jnp.where(stat_iota == 2 * term + half, part, stats)
        stage[owner, 0:256, :] = mean.astype(BF)
        stage[owner, 256:272, :] = stats.astype(BF)

        @pl.when(owner != me)
        def _():
            s_copy(owner, me).start()

    @after.append
    def _():
        @pl.loop(1, PLANE)
        def _(i):
            s_copy(lax.rem(me + i, PLANE), me).wait_send()

    @pl.loop(0, PLANE // 2)
    def _(i):
        for batch in range(2):

            @pl.when(i == 3 + 2 * batch)
            def _():
                @pl.loop(1, 4)
                def _(k):
                    g_copy(lax.rem(row_y + k, 4), row_y, batch).wait_recv()
                    k_copy(z, lax.rem(row_y + k, 4), batch).start()

        step_x = lax.rem(lax.div(i, 2) + 1, 4)
        request, group_a = moved(sign, step_x, 2 + lax.rem(i, 2))
        group_b = moved(sign, step_x, 1 - lax.rem(i, 2))[1]
        score(request, group_a, scores_a)
        score(request, group_b, scores_b)
        level_a, total_a = soften(request, scores_a, probs_a)
        finish(request * 4 + group_a, request, probs_a, level_a, total_a)
        level_b, total_b = soften(request, scores_b, probs_b)
        finish(request * 4 + group_b, request, probs_b, level_b, total_b)

    recv[me] = stage[me]

    @pl.loop(1, PLANE)
    def _(i):
        s_copy(me, lax.rem(me + i, PLANE)).wait_recv()

    terms = recv[:, 256:272, :].astype(F32)
    term_iota = lax.broadcasted_iota(jnp.int32, (16, 16, 128), 1)
    columns = []
    for half in range(2):
        mine = jnp.logical_and(term_iota < 6, lax.rem(term_iota, 2) == half)
        level = jnp.sum(jnp.where(mine, terms, 0.0), axis=1)
        weight = jnp.exp2(level - jnp.max(level, axis=0, keepdims=True))
        weight = weight / jnp.sum(weight, axis=0, keepdims=True)
        padded = jnp.concatenate([weight, jnp.zeros((112, 128), F32)], axis=0)
        columns.append(jnp.transpose(padded))
    weights = jnp.concatenate(columns, axis=0)
    merged = jnp.zeros((256, 128), F32)
    for source in range(PLANE):
        merged = merged + weights[:, source : source + 1] * recv[source, 0:256, :].astype(F32)
    split[...] = merged.reshape(16, 16, 128)
    for head in range(16):
        flat[:, head * 128 : head * 128 + 128] = split[:, head, :].astype(BF)

    def a_copy(source, target):
        return remote(
            flat,
            abuf.at[rows16(source), :],
            a_send.at[target],
            a_recv.at[source],
            (z, c, target * 4 + row_y),
        )

    @pl.loop(1, 4)
    def _(i):
        a_copy(row_x, lax.rem(row_x + i, 4)).start()

    abuf[rows16(row_x), :] = flat[...]

    @after.append
    def _():
        @pl.loop(1, 4)
        def _(i):
            a_copy(row_x, lax.rem(row_x + i, 4)).wait_send()

    @pl.loop(1, DEPTH)
    def _(i):
        m_copy(lax.rem(z + i, DEPTH), z).wait_recv()

    meta = jnp.sum(mbuf[...], axis=0)
    expert_iota = lax.broadcasted_iota(jnp.int32, (16, 128), 0).astype(F32)
    expert_iota = expert_iota + (z * PLANE).astype(F32)
    named = jnp.zeros((16, 128), F32)
    weight = jnp.zeros((16, 128), F32)
    for k in range(8):
        hit = meta[k : k + 1, :] == expert_iota
        named = named + jnp.where(hit, 1.0, 0.0)
        weight = weight + jnp.where(hit, meta[8 + k : 9 + k, :], 0.0)
    from_row = lax.broadcasted_iota(jnp.int32, (128, 128), 0)
    to_row = lax.broadcasted_iota(jnp.int32, (128, 128), 1)
    same = lax.div(from_row, 16) == lax.div(to_row, 16)
    earlier = jnp.where(jnp.logical_and(same, from_row < to_row), 1.0, 0.0).astype(BF)
    rank = jnp.dot(named.astype(BF), earlier, preferred_element_type=F32)
    slot = 2.0 * lax.div(lax.broadcasted_iota(jnp.int32, (16, 128), 1), 16).astype(F32) + rank
    slot = jnp.where(named > 0.5, slot, -1.0)
    slot_iota = lax.broadcasted_iota(jnp.int32, (16, 16, 128), 1).astype(F32)
    chosen = slot[:, None, :] == slot_iota
    placing = jnp.where(chosen, 1.0, 0.0).reshape(256, 128).astype(BF)
    scaled = jnp.where(chosen, weight[:, None, :], 0.0).reshape(256, 128)
    turned = jnp.transpose(scaled)
    turned_high = turned.astype(BF)
    turned_low = (turned - turned_high.astype(F32)).astype(BF)

    @pl.loop(1, 4)
    def _(i):
        k_copy(z + 1, lax.rem(row_y + i, 4), 0).wait_recv()
        k_copy(z + 1, lax.rem(row_y + i, 4), 1).wait_recv()

    @pl.loop(1, 4)
    def _(i):
        a_copy(lax.rem(row_x + i, 4), row_x).wait_recv()

    gathered = abuf[...]
    for part in range(4):
        columns = jnp.dot(gathered, w_ref[part], preferred_element_type=F32)
        pstage[:, :, part * 128 : part * 128 + 128] = columns.reshape(4, 16, 128)
    own_side = lax.div(row_x, 2)

    def p_copy(source_core, source, target):
        return remote(
            pstage.at[target],
            pbuf.at[source_core, lax.rem(source, 2)],
            p_send.at[target],
            p_recv.at[source_core, lax.rem(source, 2)],
            (z, lax.div(source, 2), target * 4 + row_y),
        )

    @pl.loop(1, 4)
    def _(i):
        p_copy(c, row_x, lax.rem(row_x + i, 4)).start()

    @pl.when(own_side != c)
    def _():
        p_copy(c, row_x, row_x).start()

    @pl.when(own_side == c)
    def _():
        pbuf[c, lax.rem(row_x, 2)] = pstage[row_x]

    @after.append
    def _():
        @pl.loop(1, 4)
        def _(i):
            p_copy(c, row_x, lax.rem(row_x + i, 4)).wait_send()

        @pl.when(own_side != c)
        def _():
            p_copy(c, row_x, row_x).wait_send()

    @pl.loop(0, 2)
    def _(i):
        p_copy(other, c * 2 + i, row_x).wait_recv()

        @pl.when(c * 2 + i != row_x)
        def _():
            p_copy(c, c * 2 + i, row_x).wait_recv()

    mine = pl.ds(pl.multiple_of(c * 1024, 1024), 1024)
    theirs = pl.ds(pl.multiple_of(other * 1024, 1024), 1024)
    square = jnp.zeros((16, 128), F32)
    for part in range(8):
        cols = pl.ds(pl.multiple_of(c * 1024 + part * 128, 128), 128)
        inner = slice(part % 4 * 128, part % 4 * 128 + 128)
        arrived = pbuf[0, part // 4, :, inner] + pbuf[1, part // 4, :, inner]
        hidden = res_ref[:, cols].astype(F32) + arrived
        hid_ref[:, part * 128 : part * 128 + 128] = hidden
        square = square + hidden * hidden
    sq_stage[...] = square
    sq_copy = remote(sq_stage, sq_recv, sq_sems.at[0], sq_sems.at[1], (z, other, me))
    sq_copy.start()
    after.append(sq_copy.wait_send)
    scaled_hidden = hid_ref[...] * gain_ref[:, mine]
    sq_copy.wait_recv()
    square = square + sq_recv[...]
    mean_square = jnp.sum(square, axis=1, keepdims=True) * (1.0 / 2048.0)
    norm_ref[...] = (scaled_hidden * lax.rsqrt(mean_square + norm_epsilon)).astype(BF)

    def z_copy(source, target):
        return remote(
            norm_ref, zbuf.at[rows16(source), :], z_send.at[target], z_recv.at[source], (target, c, me)
        )

    @pl.loop(1, DEPTH)
    def _(i):
        z_copy(z, lax.rem(z + far_first(i), DEPTH)).start()

    @after.append
    def _():
        @pl.loop(1, DEPTH)
        def _(i):
            z_copy(z, lax.rem(z + i, DEPTH)).wait_send()

    zbuf[rows16(z), :] = norm_ref[...]
    w_copy(1).wait()

    @pl.loop(0, 2048 // TURN)
    def _(i):
        rows = pl.ds(pl.multiple_of(i * TURN, TURN), TURN)
        for side in range(2):
            in_ref[rows, side * 384 : side * 384 + 384] = in_raw[rows, side, :]

    w_copy(2).wait()

    @pl.loop(1, DEPTH)
    def _(i):
        z_copy(lax.rem(z + i, DEPTH), z).wait_recv()

    xstage[...] = jnp.dot(placing, zbuf[...], preferred_element_type=F32).astype(BF)

    def x_copy(step):
        target = partner(step)
        return remote(
            xstage.at[rows16(target), :],
            xbuf.at[rows16(step), mine],
            x_send.at[step],
            x_recv.at[step],
            (z, c, target),
        )

    def h_copy(step, columns):
        block = xbuf.at[rows16(step), columns]
        return remote(block, block, h_send.at[step], h_recv.at[step], (z, other, me))

    def y_copy(half):
        rows = pl.ds(half * 128, 128)
        return remote(
            ystage.at[rows, :], ybuf.at[rows, :], y_send.at[half], y_recv.at[half], (z, other, me)
        )

    def r_copy(step, expert):
        return remote(
            rstage.at[rows16(step), :],
            rbuf.at[rows16(expert), :],
            r_send.at[step],
            r_recv.at[step],
            (z, c, origin(step)),
        )

    def forward(start, stop):
        @pl.loop(start, stop)
        def _(i):
            x_copy(i).wait_recv()
            h_copy(i, mine).start()

    def evaluate(half):
        @pl.loop(8 * half, 8 * half + 8)
        def _(i):
            h_copy(i, theirs).wait_recv()

        rows = slice(128 * half, 128 * half + 128)
        gate_up = jnp.dot(xbuf[rows, :], in_ref[...], preferred_element_type=F32)
        gate = gate_up[:, :384]
        active = (gate / (1.0 + jnp.exp(-gate)) * gate_up[:, 384:]).astype(BF)
        partial = jnp.dot(active, down_ref[:, theirs], preferred_element_type=F32)
        ystage[rows, :] = partial.astype(BF)
        y_copy(half).start()
        own_ref[rows, :] = jnp.dot(active, down_ref[:, mine], preferred_element_type=F32)

    def give_back(half):
        rows = slice(128 * half, 128 * half + 128)
        y_copy(half).wait_recv()
        rstage[rows, :] = (own_ref[rows, :] + ybuf[rows, :].astype(F32)).astype(BF)

        @pl.loop(max(1, 8 * half), 8 * half + 8)
        def _(i):
            r_copy(i, me).start()

    @pl.loop(1, PLANE)
    def _(i):
        x_copy(i).start()

    @after.append
    def _():
        @pl.loop(1, PLANE)
        def _(i):
            x_copy(i).wait_send()

    @after.append
    def _():
        @pl.loop(0, PLANE)
        def _(i):
            h_copy(i, mine).wait_send()

    xbuf[0:16, mine] = xstage[rows16(me), :]
    h_copy(0, mine).start()
    forward(1, 8)
    evaluate(0)
    forward(8, PLANE)
    give_back(0)
    after.append(y_copy(0).wait_send)
    after.append(y_copy(1).wait_send)
    @after.append
    def _():
        @pl.loop(1, PLANE)
        def _(i):
            r_copy(i, me).wait_send()

    rbuf[rows16(me), :] = rstage[0:16, :]
    evaluate(1)
    give_back(1)

    @pl.loop(1, PLANE)
    def _(i):
        r_copy(i, partner(i)).wait_recv()

    mixed = jnp.dot(turned_high, rbuf[...], preferred_element_type=F32)
    mixed = mixed + jnp.dot(turned_low, rbuf[...], preferred_element_type=F32)
    cstage[...] = mixed.astype(BF)

    def c_copy(source, target):
        return remote(
            cstage.at[rows16(target), :],
            cbuf.at[source],
            c_send.at[target],
            c_recv.at[source],
            (target, c, me),
        )

    @pl.loop(1, DEPTH)
    def _(i):
        c_copy(z, lax.rem(z + far_first(i), DEPTH)).start()

    @after.append
    def _():
        @pl.loop(1, DEPTH)
        def _(i):
            c_copy(z, lax.rem(z + i, DEPTH)).wait_send()

    cbuf[z] = cstage[rows16(z), :]

    @pl.loop(1, DEPTH)
    def _(i):
        c_copy(lax.rem(z + i, DEPTH), z).wait_recv()

    total = hid_ref[...]
    for source in range(DEPTH):
        total = total + cbuf[source].astype(F32)
    out_ref[...] = total.astype(BF)

    for settle in after:
        settle()


def dma(*shape):
    return pltpu.SemaphoreType.DMA(shape)


def layer(span, *operands):
    specs = [pl.BlockSpec(memory_space=pltpu.VMEM)] * 13
    for held in (3, 4, 7, 11, 12):
        specs[held] = pl.BlockSpec(memory_space=pl.ANY)
    specs[5] = pl.BlockSpec(memory_space=pltpu.SMEM)
    keys = span + 128
    return pl.pallas_call(
        functools.partial(layer_kernel, span),
        out_shape=jax.ShapeDtypeStruct((16, 1024), BF),
        in_specs=specs,
        out_specs=pl.BlockSpec(memory_space=pltpu.VMEM),
        scratch_shapes=[
            pltpu.VMEM((2, 4, 2 * span, 128), BF),
            pltpu.VMEM((2 * TILE, 128), F32),
            pltpu.VMEM((4, keys, 256), BF),
            pltpu.VMEM((4, keys, 256), BF),
            pltpu.VMEM((4, 8, keys), F32),
            pltpu.VMEM((4, 4, 256, 128), BF),
            pltpu.VMEM((256, keys), F32),
            pltpu.VMEM((256, keys), F32),
            pltpu.VMEM((256, keys), BF),
            pltpu.VMEM((256, keys), BF),
            pltpu.VMEM((PLANE, 272, 128), BF),
            pltpu.VMEM((PLANE, 272, 128), BF),
            pltpu.VMEM((16, 16, 128), F32),
            pltpu.VMEM((16, 2048), BF),
            pltpu.VMEM((64, 2048), BF),
            pltpu.VMEM((4, 2048, 128), BF),
            pltpu.VMEM((4, 16, 512), F32),
            pltpu.VMEM((2, 2, 16, 512), F32),
            pltpu.VMEM((16, 1024), F32),
            pltpu.VMEM((16, 128), F32),
            pltpu.VMEM((16, 128), F32),
            pltpu.VMEM((16, 1024), BF),
            pltpu.VMEM((2048, 2, 384), BF),
            pltpu.VMEM((2048, 768), BF),
            pltpu.VMEM((384, 2048), BF),
            pltpu.VMEM((16, 128), F32),
            pltpu.VMEM((128, 1024), BF),
            pltpu.VMEM((DEPTH, 16, 128), F32),
            pltpu.VMEM((256, 1024), BF),
            pltpu.VMEM((256, 2048), BF),
            pltpu.VMEM((256, 1024), F32),
            pltpu.VMEM((256, 1024), BF),
            pltpu.VMEM((256, 1024), BF),
            pltpu.VMEM((256, 1024), BF),
            pltpu.VMEM((256, 1024), BF),
            pltpu.VMEM((128, 1024), BF),
            pltpu.VMEM((DEPTH, 16, 1024), BF),
            dma(2, 4),
            dma(3),
            dma(2, 4),
            dma(2, 4),
            dma(2, 4),
            dma(2, 4),
            dma(PLANE),
            dma(PLANE),
            dma(4),
            dma(4),
            dma(2, 4),
            dma(2, 4),
            dma(2, 4),
            dma(2, 4),
            dma(4),
            dma(2, 2),
            dma(2),
            dma(DEPTH),
            dma(DEPTH),
            dma(DEPTH),
            dma(DEPTH),
            dma(PLANE),
            dma(PLANE),
            dma(PLANE),
            dma(PLANE),
            dma(2),
            dma(2),
            dma(PLANE),
            dma(PLANE),
            dma(DEPTH),
            dma(DEPTH),
        ],
        compiler_params=pltpu.CompilerParams(
            collective_id=0, has_side_effects=True, vmem_limit_bytes=VMEM_LIMIT
        ),
    )(*operands)


def local(
    queries,
    new_keys,
    new_values,
    key_cache,
    value_cache,
    lengths,
    residual,
    out_weight,
    norm_gain,
    route_ids,
    route_weights,
    expert_in,
    expert_out,
):
    requests, span = key_cache.shape[:2]
    return layer(
        span,
        queries.reshape(requests, 64, 128),
        new_keys.reshape(requests, 8, 128),
        new_values.reshape(requests, 8, 128),
        key_cache.reshape(requests, 2 * span, 128),
        value_cache.reshape(requests, 2 * span, 128),
        lengths,
        residual,
        out_weight,
        norm_gain.reshape(1, -1),
        route_ids.T,
        route_weights.T,
        expert_in.reshape(2048, 2, 384),
        expert_out.reshape(384, 2048),
    )


def solution(mesh):
    return jax.shard_map(
        local,
        mesh=mesh,
        in_specs=(
            P("req", "exp", "head", None),
            P("req", "exp", "head", None),
            P("req", "exp", "head", None),
            P("req", "exp", "head", None),
            P("req", "exp", "head", None),
            P("req"),
            P(("req", "exp"), None),
            P("head", "exp"),
            P(),
            P(("req", "exp"), None),
            P(("req", "exp"), None),
            P(("req", "exp"), None, None, "head"),
            P(("req", "exp"), "head", None),
        ),
        out_specs=P(("req", "exp"), "head"),
        check_vma=False,
    )
```
